128 devices in a mesh: shard: 4 (over y_lo, core), replica: 32 (over z, x, y_hi).
Axes of the slice: x: 4, y: 4 (y_hi: 2, y_lo: 2; y = y_hi * 2 + y_lo), z: 4, core: 2. Of those that a mesh axis runs over, the one named last changes fastest.
Arguments:
- tokens: bfloat16 [128, 384, 960], P(('shard', 'replica')), may hold values from -6 to 6
- lengths: int32 [128, 4], P(('shard', 'replica')), may hold values from 0 to 384, as said below
- norm_attn: bfloat16 [960], P('shard'), may hold values from 0.5 to 1.5
- w_query: bfloat16 [960, 960], P('shard'), may hold values from -0.1875 to 0.1875
- w_key: bfloat16 [960, 320], P('shard'), may hold values from -0.1875 to 0.1875
- w_value: bfloat16 [960, 320], P('shard'), may hold values from -0.1875 to 0.1875
- w_out: bfloat16 [960, 960], P('shard'), may hold values from -2 to 2
- norm_mlp: bfloat16 [960], P('shard'), may hold values from 0.5 to 1.5
- w_gate: bfloat16 [960, 2560], P('shard'), may hold values from -0.1875 to 0.1875
- w_up: bfloat16 [960, 2560], P('shard'), may hold values from -0.1875 to 0.1875
- w_down: bfloat16 [2560, 960], P('shard'), may hold values from -0.125 to 0.125
- cotangent: bfloat16 [128, 384, 960], P(('shard', 'replica')), may hold values from -6 to 6
Outputs:
- out: bfloat16 [128, 384, 960], P(('shard', 'replica'))
- grad_in: float32 [128, 384, 960], P(('shard', 'replica'))
- grad_norm_attn: float32 [960], P('shard')
- grad_query: float32 [960, 960], P('shard')
- grad_key: float32 [960, 320], P('shard')
- grad_value: float32 [960, 320], P('shard')
- grad_out_proj: float32 [960, 960], P('shard')
- grad_norm_mlp: float32 [960], P('shard')
- grad_gate: float32 [960, 2560], P('shard')
- grad_up: float32 [960, 2560], P('shard')
- grad_down: float32 [2560, 960], P('shard')
The draws below stay inside these ranges and needn't reach their ends.
Inputs may be any that keep to these rules, and one draw needn't show every extreme that they name: Row g lists the lengths of the sequences packed in order into pack g's 384 slots, zeros for unused entries; each row sums to 384.
All inputs are finite; a program needn't handle non-finite values.
Results may differ from the reference program's by a relative error of at most 0.028.
Values may be sent and summed in bfloat16 or wider, within the bound.
No kernel may reach another device: no remote copies, remote signals or barrier semaphores. Data moves between devices by JAX's collectives and lax.ppermute only.
A program may use at most 256 MiB of HBM per device.

```python
import jax
import jax.numpy as jnp
from jax import lax

D = 960
HEADS = 15
KV_HEADS = 5
HEAD_DIM = 64
FF = 2560
SEQS = 4
GROUPS = 128
GROUP_TOK = 384


def draw_lengths(key, part):
    key = jax.random.fold_in(key, 11)
    first_key, cut_key, pick_key = jax.random.split(key, 3)
    first = jax.random.randint(first_key, (GROUPS,), 3 * GROUP_TOK // 4 + 1, GROUP_TOK + 1)
    chosen = jax.random.randint(pick_key, (), 0, GROUPS)
    first = jnp.where(jnp.arange(GROUPS) == chosen, GROUP_TOK, first).astype(jnp.int32)
    remain = (GROUP_TOK - first).astype(jnp.int32)
    raw = jax.random.randint(cut_key, (GROUPS, SEQS - 2), 0, 1 << 20)
    cuts = jnp.sort(raw % (remain[:, None] + 1), axis=1).astype(jnp.int32)
    edges = jnp.concatenate([jnp.zeros((GROUPS, 1), jnp.int32), cuts, remain[:, None]], axis=1)
    rest = edges[:, 1:] - edges[:, :-1]
    return jnp.concatenate([first[:, None], rest], axis=1).astype(jnp.int32)


def shard_levels(stream_key, shape, cuts, smallest, top_value):
    level, own = 1.0, jax.random.fold_in(stream_key, 6)
    for dim, blocks in cuts:
        steps = jnp.exp(jax.random.uniform(jax.random.fold_in(own, dim), (blocks,), jnp.float32, smallest / len(cuts), top_value / len(cuts)))
        level = level * jnp.repeat(steps, shape[dim] // blocks).reshape([-1 if axis == dim else 1 for axis in range(len(shape))])
    return level


def normal_values(stream_key, dims, width, bound, cuts=(), kind=jnp.bfloat16):
    array = width * jax.random.normal(stream_key, dims, jnp.float32)
    if cuts:
        array = array * shard_levels(stream_key, dims, cuts, -0.22, 0.18)
    return jnp.clip(array, -bound, bound).astype(kind)


def setup_inputs(seed: int = 0) -> dict:
    seeds = jax.random.split(jax.random.key(seed), 13)
    tokens = normal_values(seeds[0], (GROUPS, GROUP_TOK, D), 1.0, 6.0, ((0, 128),))
    lengths = draw_lengths(jax.random.fold_in(seeds[12], 71), 0)
    norm_attn = jnp.clip(1.0 + 0.1 * jax.random.normal(seeds[2], (D,), jnp.float32), 0.5, 1.5).astype(jnp.bfloat16)
    w_query = normal_values(seeds[3], (D, HEADS * HEAD_DIM), D ** -0.5, 0.1875, ((0, 4),))
    w_key = normal_values(seeds[4], (D, KV_HEADS * HEAD_DIM), D ** -0.5, 0.1875, ((0, 4),))
    w_value = normal_values(seeds[5], (D, KV_HEADS * HEAD_DIM), D ** -0.5, 0.1875, ((0, 4),))
    w_out = normal_values(seeds[6], (HEADS * HEAD_DIM, D), (max(D * 4 // GROUP_TOK, 1)) ** -0.5, 2.0, ((0, 4),))
    norm_mlp = jnp.clip(1.0 + 0.1 * jax.random.normal(seeds[7], (D,), jnp.float32), 0.5, 1.5).astype(jnp.bfloat16)
    w_gate = normal_values(seeds[8], (D, FF), D ** -0.5, 0.1875, ((0, 4),))
    w_up = normal_values(seeds[9], (D, FF), D ** -0.5, 0.1875, ((0, 4),))
    w_down = normal_values(seeds[10], (FF, D), FF ** -0.5, 0.125, ((0, 4),))
    cotangent = normal_values(seeds[11], (GROUPS, GROUP_TOK, D), 1.0, 6.0, ((0, 128),))
    return dict(tokens=tokens, lengths=lengths, norm_attn=norm_attn, w_query=w_query, w_key=w_key, w_value=w_value, w_out=w_out, norm_mlp=norm_mlp, w_gate=w_gate, w_up=w_up, w_down=w_down, cotangent=cotangent)


@jax.custom_vjp
def low(v):
    return lax.optimization_barrier(v.astype(jnp.bfloat16)).astype(jnp.float32)

@jax.custom_vjp
def low_back(v):
    return v

def low_keep(v):
    return (low(v), None)

def low_pass(kept, grad):
    return (grad,)

def back_keep(v):
    return (v, None)

def back_low(kept, grad):
    return (low(grad),)
low.defvjp(low_keep, low_pass)
low_back.defvjp(back_keep, back_low)
EPS = 1e-05
BASE = 100000.0
MASKED = -1e+30
HIGH = lax.Precision.HIGHEST

def slots_of(lengths_row):
    slots = jnp.arange(GROUP_TOK, dtype=jnp.int32)
    ends = jnp.cumsum(lengths_row).astype(jnp.int32)
    reached = slots[:, None] >= ends[None, :]
    segment = lax.optimization_barrier(jnp.sum(reached.astype(jnp.int32), axis=1))
    start = lax.optimization_barrier(jnp.max(jnp.where(reached, ends[None, :], 0), axis=1)).astype(jnp.int32)
    return (segment, slots - start, slots)

def rotate(values, position):
    half = HEAD_DIM // 2
    freq = BASE ** (-jnp.arange(half, dtype=jnp.float32) * 2.0 / HEAD_DIM)
    angle = position.astype(jnp.float32)[:, None] * freq[None, :]
    cosine = jnp.cos(angle)[:, None, :]
    sine = jnp.sin(angle)[:, None, :]
    first = values[..., :half]
    second = values[..., half:]
    return jnp.concatenate([first * cosine - second * sine, second * cosine + first * sine], axis=-1)

def rms(values, gain):
    return values * lax.rsqrt(lax.optimization_barrier(jnp.mean(values * values, axis=-1, keepdims=True)) + EPS) * gain

def layer(x, segment, position, slots, weights):
    gain_attn, wq, wk, wv, wo, gain_mlp, wg, wu, wd = weights
    group_size = HEADS // KV_HEADS
    a = low(rms(x, gain_attn))
    query = low(rotate(low_back(jnp.dot(a, wq, precision=HIGH)).reshape(GROUP_TOK, HEADS, HEAD_DIM), position))
    keys = low(rotate(low_back(jnp.dot(a, wk, precision=HIGH)).reshape(GROUP_TOK, KV_HEADS, HEAD_DIM), position))
    values = low(low_back(jnp.dot(a, wv, precision=HIGH))).reshape(GROUP_TOK, KV_HEADS, HEAD_DIM)
    query = query.reshape(GROUP_TOK, KV_HEADS, group_size, HEAD_DIM)
    allowed = (segment[:, None] == segment[None, :]) & (slots[None, :] <= slots[:, None])
    scores = low_back(jnp.einsum('tkgd,skd->kgts', query, keys, precision=HIGH) * 0.125)
    scores = jnp.where(allowed, scores, MASKED)
    top = lax.optimization_barrier(jnp.max(scores, axis=-1, keepdims=True))
    expo = jnp.exp(scores - top)
    prob = low(expo / lax.optimization_barrier(jnp.sum(expo, axis=-1, keepdims=True)))
    attended = jnp.einsum('kgts,skd->tkgd', prob, values, precision=HIGH).reshape(GROUP_TOK, HEADS * HEAD_DIM)
    attended = low(low_back(attended))
    hidden = x + low_back(jnp.dot(attended, wo, precision=HIGH))
    normed = low(rms(hidden, gain_mlp))
    gate = low_back(jnp.dot(normed, wg, precision=HIGH))
    upper = low_back(jnp.dot(normed, wu, precision=HIGH))
    act = low(jax.nn.silu(gate) * upper)
    return hidden + low_back(jnp.dot(act, wd, precision=HIGH))

def reference(tokens, lengths, norm_attn, w_query, w_key, w_value, w_out, norm_mlp, w_gate, w_up, w_down, cotangent):
    weights = tuple((w.astype(jnp.float32) for w in (norm_attn, w_query, w_key, w_value, w_out, norm_mlp, w_gate, w_up, w_down)))
    inputs = tokens.astype(jnp.float32)

    def forward(inputs, weights):

        def one_group(carry, item):
            x, row = item
            segment, position, slots = slots_of(row)
            return (carry, layer(x, segment, position, slots, weights))
        _, result = lax.scan(jax.checkpoint(one_group), jnp.zeros((), jnp.float32), (inputs, lengths))
        return result
    result, pull = jax.vjp(forward, inputs, weights)
    grad_inputs, grad_weights = pull(cotangent.astype(jnp.float32))
    return (result.astype(jnp.bfloat16), grad_inputs, grad_weights[0], grad_weights[1], grad_weights[2], grad_weights[3], grad_weights[4], grad_weights[5], grad_weights[6], grad_weights[7], grad_weights[8])
```

```python
import jax
import jax.numpy as jnp
from jax import lax
from jax.sharding import Mesh
from jax.sharding import PartitionSpec as P

HEADS = 15
KV_HEADS = 5
HEAD_DIM = 64
SHARD = ("y_lo", "core")
EVERY = ("y_lo", "core", "z", "x", "y_hi")


EPS = 1e-05
BASE = 100000.0
MASKED = -1e30


def swap_cores(value):
    return lax.ppermute(value, "core", [(0, 1), (1, 0)])


def shift_ring(value, axis, by):
    return lax.ppermute(value, axis, [(i, (i + by) % 4) for i in range(4)])


def shift_y(value, by):
    place = [(y % 2) * 2 + y // 2 for y in range(4)]
    return lax.ppermute(value, ("y_lo", "y_hi"), [(place[y], place[(y + by) % 4]) for y in range(4)])


def halves(value):
    half = value.shape[0] // 2
    return value[:half], value[half:]


def ring_gather(value, axis):
    before = shift_ring(value, axis, 1)
    after = shift_ring(value, axis, -1)
    top = shift_ring(halves(before)[0], axis, 1)
    bottom = shift_ring(halves(after)[1], axis, -1)
    return value, before, after, jnp.concatenate([top, bottom])


def ring_scatter(pieces, axis):
    own, before, after, across = pieces
    top, bottom = halves(across)
    got_top = shift_ring(top, axis, 1)
    got_bottom = shift_ring(bottom, axis, -1)
    after_top, after_bottom = halves(after)
    before_top, before_bottom = halves(before)
    after = jnp.concatenate([add_low(after_top, got_top), after_bottom])
    before = jnp.concatenate([before_top, add_low(before_bottom, got_bottom)])
    return add_low(own, shift_ring(after, axis, 1), shift_ring(before, axis, -1))


def add_low(*terms):
    total = terms[0].astype(jnp.float32)
    for term in terms[1:]:
        total = total + term.astype(jnp.float32)
    return total.astype(jnp.bfloat16)


def take(value, axis_name, by, parts, dim):
    size = value.shape[dim] // parts
    place = lax.rem(lax.axis_index(axis_name) + by + parts, parts)
    return lax.dynamic_slice_in_dim(value, place * size, size, dim)


def ring_pieces(value, axis, dim):
    return tuple(take(value, axis, by, 4, dim) for by in (0, -1, 1, 2))


def ring_joined(pieces, axis, dim):
    value = jnp.concatenate([pieces[k] for k in (0, 2, 3, 1)], axis=dim)
    size = pieces[0].shape[dim]
    lengths = list(value.shape)
    out = jnp.zeros(lengths, value.dtype)
    place = lax.axis_index(axis)
    for k, by in enumerate((0, -1, 1, 2)):
        at = lax.rem(place + by + 4, 4) * size
        out = lax.dynamic_update_slice_in_dim(out, pieces[k], at, dim)
    return out


def placed(pieces):
    me = lax.axis_index("y_lo") * 2 + lax.axis_index("core")
    rows, columns = pieces[0][1].shape
    out = jnp.zeros((4, rows, columns), pieces[0][1].dtype)
    for flip, piece in pieces:
        at = lax.bitwise_xor(me, jnp.int32(flip))
        out = lax.dynamic_update_slice(out, piece[None], (at, 0, 0))
    return out.reshape(4 * rows, columns)


def far_direct(shard):
    top, bottom = halves(shard)
    return jnp.concatenate([shift_y(top, 1), shift_y(bottom, -1)])


def far_by_ring(shard, axis, dim):
    piece = take(shard, axis, 0, 4, dim)
    return ring_joined(ring_gather(far_direct(piece), axis), axis, dim)


def all_rows(shard, far):
    return placed(((0, shard), (1, swap_cores(shard)), (2, far), (3, swap_cores(far))))


def of_core(value, other):
    rows, columns = value.shape
    core = lax.axis_index("core")
    core = 1 - core if other else core
    split = value.reshape(rows, 2, 2, columns // 4)
    return lax.dynamic_index_in_dim(split, core, 2, keepdims=False).reshape(rows, columns // 2)


def reduced(total, first, second, dims):
    low = lax.axis_index("y_lo")
    mine = lax.dynamic_index_in_dim(total, low, 0, keepdims=False)
    theirs = lax.dynamic_index_in_dim(total, 1 - low, 0, keepdims=False)
    part = add_low(mine, far_direct(theirs))
    part = ring_scatter(ring_pieces(part, first, dims[0]), first)
    part = ring_scatter(ring_pieces(part, second, dims[1]), second)
    part = add_low(part, lax.ppermute(part, "y_hi", [(0, 1), (1, 0)]))
    part = ring_joined(ring_gather(part, second), second, dims[1])
    return ring_joined(ring_gather(part, first), first, dims[0]).astype(jnp.float32)


def chip_sum(left, right):
    sent = swap_cores(mult_tn(of_core(left, True), right).astype(jnp.bfloat16))
    total = mult_tn(of_core(left, False), right) + sent.astype(jnp.float32)
    total = total.astype(jnp.bfloat16)
    return total.reshape(2, total.shape[0] // 2, total.shape[1])


def slots_of(lengths_row, total):
    slots = jnp.arange(total, dtype=jnp.int32)
    ends = jnp.cumsum(lengths_row)
    reached = slots[:, None] >= ends[None, :]
    segment = jnp.sum(reached.astype(jnp.int32), axis=1)
    start = jnp.max(jnp.where(reached, ends[None, :], 0), axis=1)
    return (segment, slots - start, slots)


def rotate(values, position, sign):
    half = values.shape[-1] // 2
    freq = BASE ** (-jnp.arange(half, dtype=jnp.float32) * 2.0 / values.shape[-1])
    angle = position.astype(jnp.float32)[:, None] * freq[None, :]
    cosine = jnp.cos(angle)[:, None, :]
    sine = sign * jnp.sin(angle)[:, None, :]
    first = values[..., :half]
    second = values[..., half:]
    return jnp.concatenate(
        [first * cosine - second * sine, second * cosine + first * sine], axis=-1
    )


def normed(values, gain):
    scale = lax.rsqrt(jnp.mean(values * values, axis=-1, keepdims=True) + EPS)
    return (values * scale * gain, scale)


def norm_back(values, scale, gain, grad):
    inner = grad * gain
    cubed = scale * scale * scale
    d_values = scale * inner - values * cubed * jnp.mean(values * inner, axis=-1, keepdims=True)
    d_gain = jnp.sum(grad * values * scale, axis=0)
    return (d_values, d_gain)


def mult(left, right):
    return jnp.dot(left, right, preferred_element_type=jnp.float32)


def mult_tn(left, right):
    return lax.dot_general(
        left, right, (((0,), (0,)), ((), ())), preferred_element_type=jnp.float32
    )


def mult_nt(left, right):
    return lax.dot_general(
        left, right, (((1,), (1,)), ((), ())), preferred_element_type=jnp.float32
    )


def body(
    tokens,
    lengths,
    norm_attn,
    w_query,
    w_key,
    w_value,
    w_out,
    norm_mlp,
    w_gate,
    w_up,
    w_down,
    cotangent,
):
    local = tokens.shape[1]
    width = tokens.shape[2]
    group_size = HEADS // KV_HEADS
    gains = jnp.stack([norm_attn, norm_mlp])
    gains = all_rows(gains, shift_y(gains, 1)).reshape(4, 2, -1).transpose(1, 0, 2)
    gain_attn, gain_mlp = gains.reshape(2, width)
    first = jnp.concatenate([w_query, w_key, w_value, w_out], axis=1)
    first = all_rows(first, far_direct(first))
    edges = (width, width + w_key.shape[1], width + 2 * w_key.shape[1])
    wq, wk, wv, wo = jnp.split(first, edges, axis=1)
    wg = all_rows(w_gate, far_by_ring(w_gate, "z", 1))
    wu = all_rows(w_up, far_by_ring(w_up, "x", 1))
    wd = all_rows(w_down, far_direct(w_down))
    gain_attn = gain_attn.astype(jnp.float32)
    gain_mlp = gain_mlp.astype(jnp.float32)
    segment, position, slots = slots_of(lengths[0], local)
    allowed = (segment[:, None] == segment[None, :]) & (slots[None, :] <= slots[:, None])
    x = tokens[0].astype(jnp.float32)
    a_full, scale_a = normed(x, gain_attn)
    a_low = a_full.astype(jnp.bfloat16)
    query = rotate(mult(a_low, wq).reshape(local, HEADS, HEAD_DIM), position, 1.0).astype(
        jnp.bfloat16
    )
    keys = rotate(mult(a_low, wk).reshape(local, KV_HEADS, HEAD_DIM), position, 1.0).astype(
        jnp.bfloat16
    )
    values = mult(a_low, wv).astype(jnp.bfloat16)
    query_heads = query.reshape(local, KV_HEADS, group_size, HEAD_DIM).transpose(1, 0, 2, 3)
    key_heads = keys.transpose(1, 0, 2)
    value_heads = values.reshape(local, KV_HEADS, HEAD_DIM).transpose(1, 0, 2)

    def head_scores(query_one, key_one):
        scores = (
            jnp.einsum("tgd,sd->gts", query_one, key_one, preferred_element_type=jnp.float32)
            * 0.125
        )
        return jnp.where(allowed[None], scores, MASKED)

    def head_forward(item):
        query_one, key_one, value_one = item
        scores = head_scores(query_one, key_one)
        top = jnp.max(scores, axis=-1, keepdims=True)
        expo = jnp.exp(scores - top)
        total_weight = jnp.sum(expo, axis=-1, keepdims=True)
        prob_low = (expo / total_weight).astype(jnp.bfloat16)
        result = jnp.einsum("gts,sd->tgd", prob_low, value_one, preferred_element_type=jnp.float32)
        return (result, top + jnp.log(total_weight))

    attended, log_total = lax.map(head_forward, (query_heads, key_heads, value_heads))
    att_low = attended.transpose(1, 0, 2, 3).reshape(local, HEADS * HEAD_DIM).astype(jnp.bfloat16)
    hidden = x + mult(att_low, wo)
    b_full, scale_b = normed(hidden, gain_mlp)
    b_low = b_full.astype(jnp.bfloat16)
    gate = mult(b_low, wg)
    upper = mult(b_low, wu)
    sigma = jax.nn.sigmoid(gate)
    silu_gate = gate * sigma
    act_low = (silu_gate * upper).astype(jnp.bfloat16)
    result = (hidden + mult(act_low, wd)).astype(jnp.bfloat16)[None]
    dy_low = cotangent[0]
    dy = dy_low.astype(jnp.float32)
    grad_down = reduced(chip_sum(act_low, dy_low), "z", "x", (0, 0))
    d_act = mult_nt(dy_low, wd)
    d_gate = (d_act * upper * sigma * (1.0 + gate * (1.0 - sigma))).astype(jnp.bfloat16)
    d_up = (d_act * silu_gate).astype(jnp.bfloat16)
    grad_gate = reduced(chip_sum(b_low, d_gate), "x", "z", (1, 0))
    grad_up = reduced(chip_sum(b_low, d_up), "z", "x", (1, 0))
    d_b = mult_nt(d_gate, wg) + mult_nt(d_up, wu)
    d_hidden_norm, grad_gain_mlp = norm_back(hidden, scale_b, gain_mlp, d_b)
    d_hidden = dy + d_hidden_norm
    d_hidden_low = d_hidden.astype(jnp.bfloat16)
    sum_out = chip_sum(att_low, d_hidden_low)
    d_att = mult_nt(d_hidden_low, wo).astype(jnp.bfloat16)
    d_att_heads = d_att.reshape(local, KV_HEADS, group_size, HEAD_DIM).transpose(1, 0, 2, 3)

    def head_backward(item):
        query_one, key_one, value_one, d_one, log_one = item
        prob = jnp.exp(head_scores(query_one, key_one) - log_one)
        prob_low = prob.astype(jnp.bfloat16)
        d_prob = jnp.einsum("tgd,sd->gts", d_one, value_one, preferred_element_type=jnp.float32)
        inner = jnp.sum(prob * d_prob, axis=-1, keepdims=True)
        d_scores = (prob * (d_prob - inner)).astype(jnp.bfloat16)
        d_query = (
            jnp.einsum("gts,sd->tgd", d_scores, key_one, preferred_element_type=jnp.float32) * 0.125
        )
        d_key = (
            jnp.einsum("gts,tgd->sd", d_scores, query_one, preferred_element_type=jnp.float32)
            * 0.125
        )
        d_value = jnp.einsum("gts,tgd->sd", prob_low, d_one, preferred_element_type=jnp.float32)
        return (d_query, d_key, d_value)

    d_query, d_keys, d_values = lax.map(
        head_backward, (query_heads, key_heads, value_heads, d_att_heads, log_total)
    )
    dq_low = rotate(d_query.transpose(1, 0, 2, 3).reshape(local, HEADS, HEAD_DIM), position, -1.0)
    dq_low = dq_low.reshape(local, HEADS * HEAD_DIM).astype(jnp.bfloat16)
    dk_low = rotate(d_keys.transpose(1, 0, 2), position, -1.0)
    dk_low = dk_low.reshape(local, KV_HEADS * HEAD_DIM).astype(jnp.bfloat16)
    dv_low = d_values.transpose(1, 0, 2).reshape(local, KV_HEADS * HEAD_DIM).astype(jnp.bfloat16)
    sum_in = chip_sum(a_low, jnp.concatenate([dq_low, dk_low, dv_low], axis=1))
    d_a = mult_nt(dq_low, wq) + mult_nt(dk_low, wk) + mult_nt(dv_low, wv)
    d_x_norm, grad_gain_attn = norm_back(x, scale_a, gain_attn, d_a)
    grad_input = (d_hidden + d_x_norm)[None]
    sums = jnp.concatenate([sum_in, sum_out], axis=2)
    own = reduced(sums, "x", "z", (1, 0))
    edges = (width, width + w_key.shape[1], width + 2 * w_key.shape[1])
    grad_query, grad_key, grad_value, grad_out_proj = jnp.split(own, edges, axis=1)
    gain_sums = lax.psum(jnp.stack([grad_gain_attn, grad_gain_mlp]), EVERY)
    me = lax.axis_index("y_lo") * 2 + lax.axis_index("core")
    rows = width // 4
    own_gains = lax.dynamic_slice_in_dim(gain_sums, me * rows, rows, 1)
    return (
        result,
        grad_input,
        own_gains[0],
        grad_query,
        grad_key,
        grad_value,
        grad_out_proj,
        own_gains[1],
        grad_gate,
        grad_up,
        grad_down,
    )


def solution(mesh):
    torus = Mesh(
        mesh.devices.reshape(2, 2, 4, 4, 2), EVERY
    )
    return jax.shard_map(
        body,
        mesh=torus,
        in_specs=(
            P(EVERY, None, None),
            P(EVERY, None),
            P(SHARD),
            P(SHARD, None),
            P(SHARD, None),
            P(SHARD, None),
            P(SHARD, None),
            P(SHARD),
            P(SHARD, None),
            P(SHARD, None),
            P(SHARD, None),
            P(EVERY, None, None),
        ),
        out_specs=(
            P(EVERY, None, None),
            P(EVERY, None, None),
            P(SHARD),
            P(SHARD, None),
            P(SHARD, None),
            P(SHARD, None),
            P(SHARD, None),
            P(SHARD),
            P(SHARD, None),
            P(SHARD, None),
            P(SHARD, None),
        ),
        check_vma=False,
    )
```

```python
import jax
import jax.numpy as jnp
from jax import lax
from jax.experimental import pallas as pl
from jax.experimental.pallas import tpu as pltpu
from jax.sharding import Mesh
from jax.sharding import PartitionSpec as P

T = 384
D = 960
FF = 2560
HEADS = 15
KV = 5
GROUP = 3
HEAD_DIM = 64
BLOCK = 128
BLOCKS = T // BLOCK
STACK = GROUP * BLOCK
QK = (HEADS + KV) * HEAD_DIM
QKV = QK + KV * HEAD_DIM
AT_QKV = 1024
PACK = AT_QKV + QKV
ROWS = D // 4
TOP = 128
UNIT = 640
EVERY = ("y_lo", "core", "z", "x", "y_hi")
SHARD = ("y_lo", "core")
EPS = 1e-05
BASE = 100000.0
MASKED = -1e30
BF = jnp.bfloat16
F32 = jnp.float32
LIMIT = 52 * 2**20

ANY = pl.BlockSpec(memory_space=pl.ANY)
VMEM = pl.BlockSpec(memory_space=pltpu.VMEM)
SMEM = pl.BlockSpec(memory_space=pltpu.SMEM)


def shape(*dims, dtype=BF):
    return jax.ShapeDtypeStruct(dims, dtype)


def mult(left, right):
    return jnp.dot(left, right, preferred_element_type=F32)


def mult_tn(left, right):
    return lax.dot_general(left, right, (((0,), (0,)), ((), ())), preferred_element_type=F32)


def mult_nt(left, right):
    return lax.dot_general(left, right, (((1,), (1,)), ((), ())), preferred_element_type=F32)


def piece_copies(pieces, full, me, rows, top, sems, columns=None):
    copies = []
    for k, (flip, start, size) in enumerate(
        ((0, 0, rows), (1, 0, rows), (2, 0, top), (2, top, rows - top), (3, 0, top), (3, top, rows - top))
    ):
        at = pl.multiple_of(lax.bitwise_xor(me, jnp.int32(flip)) * rows + start, 16)
        source, target = pieces[k], full.at[pl.ds(at, size)]
        if columns is not None:
            source, target = source.at[:, columns], full.at[pl.ds(at, size), columns]
        copies.append(pltpu.make_async_copy(source, target, sems.at[k]))
    return copies


def rope(u, cosine, sine, sign):
    lane = lax.broadcasted_iota(jnp.int32, u.shape, 1)
    turned = jnp.where(lane % HEAD_DIM < HEAD_DIM // 2, pltpu.roll(u, 96, 1), pltpu.roll(u, 32, 1))
    return u * cosine + sign * (turned * sine)


def rms_scale(v):
    return lax.rsqrt(jnp.mean(v * v, axis=-1, keepdims=True) + EPS)


def norm_back(v, gain, grad):
    scale = rms_scale(v)
    inner = grad * gain
    d_v = scale * inner - v * (scale * scale * scale) * jnp.mean(v * inner, axis=-1, keepdims=True)
    return d_v, jnp.sum(grad * v * scale, axis=0, keepdims=True)


def attention_kernel(me_ref, x_ref, gains_ref, cos_ref, sin_ref, start_ref, *refs):
    pieces, refs = refs[:6], refs[6:]
    (a_ref, q_ref, k_ref, v_ref, p0_ref, p1_ref, p2_ref, att_ref, h_ref, b_ref, w, o, bias, sems) = refs
    copies = piece_copies(pieces, w, me_ref[0], ROWS, TOP, sems)
    for copy in copies:
        copy.start()
    x = x_ref[...].astype(F32)
    a_ref[...] = (x * rms_scale(x) * gains_ref[0:1]).astype(BF)
    column = lax.broadcasted_iota(jnp.int32, (T, T), 1)
    row = lax.broadcasted_iota(jnp.int32, (T, T), 0)
    bias[...] = jnp.where((column >= start_ref[...]) & (column <= row), 0.0, MASKED)
    for copy in copies:
        copy.wait()
    a = a_ref[...]
    for c in range(QK // 256):
        wide = mult(a, w[:, AT_QKV + 256 * c : AT_QKV + 256 * (c + 1)])
        for half in range(2):
            u = rope(wide[:, 128 * half : 128 * half + 128], cos_ref[...], sin_ref[...], 1.0).astype(BF)
            for side in range(2):
                head = 4 * c + 2 * half + side
                one = u[:, HEAD_DIM * side : HEAD_DIM * (side + 1)]
                if head < HEADS:
                    for i in range(BLOCKS):
                        at = i * STACK + head % GROUP * BLOCK
                        q_ref[head // GROUP, at : at + BLOCK, :] = one[i * BLOCK : (i + 1) * BLOCK]
                else:
                    k_ref[head - HEADS] = one
    values = mult(a, w[:, AT_QKV + QK :]).astype(BF)
    for j in range(KV):
        v_ref[j] = values[:, HEAD_DIM * j : HEAD_DIM * (j + 1)]
    probs = (p0_ref, p1_ref, p2_ref)

    def one_group(j, carry):
        for i in range(BLOCKS):
            keys = (i + 1) * BLOCK
            q = q_ref[j, i * STACK : (i + 1) * STACK, :]
            scores = mult_nt(q, k_ref[j, :keys, :]) * 0.125
            part = bias[i * BLOCK : (i + 1) * BLOCK, :keys]
            scores = scores + jnp.concatenate([part] * GROUP, axis=0)
            expo = jnp.exp(scores - jnp.max(scores, axis=-1, keepdims=True))
            prob = (expo * (1.0 / jnp.sum(expo, axis=-1, keepdims=True))).astype(BF)
            probs[i][j] = prob
            o[j, i * STACK : (i + 1) * STACK, :] = mult(prob, v_ref[j, :keys, :])
        return carry

    lax.fori_loop(0, KV, one_group, 0)
    for c in range(8):
        heads = [stacked_head(o, head) for head in range(2 * c, min(2 * c + 2, HEADS))]
        wide = jnp.concatenate(heads, axis=1) if len(heads) > 1 else heads[0]
        att_ref[:, 128 * c : 128 * c + wide.shape[1]] = wide.astype(BF)
    h = x_ref[...].astype(F32) + mult(att_ref[...], w[:, :D])
    h_ref[...] = h
    b_ref[...] = (h * rms_scale(h) * gains_ref[1:2]).astype(BF)


def stacked_head(ref, head):
    at = head % GROUP * BLOCK
    return jnp.concatenate(
        [ref[head // GROUP, i * STACK + at : i * STACK + at + BLOCK, :] for i in range(BLOCKS)], axis=0
    )


CHUNK = 512


def gate_kernel(me_ref, b_ref, *refs):
    pieces, (act_ref, silu_ref, slope_ref, w, sems) = refs[:6], refs[6:]
    chunks = FF // CHUNK
    copies = []
    for c in range(chunks):
        for k in range(2):
            columns = pl.ds(k * FF + c * CHUNK, CHUNK)
            copies.append(piece_copies(pieces, w, me_ref[0], ROWS, TOP, sems.at[2 * c + k], columns))
    for group in copies:
        for copy in group:
            copy.start()
    b = b_ref[...]
    for c in range(chunks):
        at = c * CHUNK
        for group in copies[2 * c : 2 * c + 2]:
            for copy in group:
                copy.wait()
        gate = mult(b, w[:, at : at + CHUNK])
        up = mult(b, w[:, FF + at : FF + at + CHUNK])
        sigma = jax.nn.sigmoid(gate)
        silu = gate * sigma
        act_ref[:, at : at + CHUNK] = (silu * up).astype(BF)
        silu_ref[:, at : at + CHUNK] = silu.astype(BF)
        slope_ref[:, at : at + CHUNK] = (up * sigma * (1.0 + gate * (1.0 - sigma))).astype(BF)


def mlp_kernel(me_ref, act_ref, silu_ref, slope_ref, h_ref, dy_ref, gains_ref, *refs):
    down, wide, refs = refs[:6], refs[6:12], refs[12:]
    (out_ref, d_gate_ref, d_up_ref, d_h_ref, d_low_ref, d_gain_ref, wd, w, sums, sems) = refs
    first = piece_copies(down, wd, me_ref[0], FF // 4, FF // 8, sems.at[0])
    second = piece_copies(wide, w, me_ref[0], ROWS, TOP, sems.at[1])
    for copy in first + second:
        copy.start()
    for copy in first:
        copy.wait()
    dy = dy_ref[...]
    out_ref[...] = (h_ref[...] + mult(act_ref[...], wd[...])).astype(BF)
    for c in range(FF // CHUNK):
        at = c * CHUNK
        d_act = mult_nt(dy, wd[at : at + CHUNK, :])
        d_gate_ref[:, at : at + CHUNK] = (d_act * slope_ref[:, at : at + CHUNK].astype(F32)).astype(BF)
        d_up_ref[:, at : at + CHUNK] = (d_act * silu_ref[:, at : at + CHUNK].astype(F32)).astype(BF)
    for copy in second:
        copy.wait()
    sums[...] = mult_nt(d_gate_ref[...], w[:, :FF]) + mult_nt(d_up_ref[...], w[:, FF:])
    d_norm, d_gain = norm_back(h_ref[...], gains_ref[1:2], sums[...])
    d_h = dy.astype(F32) + d_norm
    d_h_ref[...] = d_h
    d_low_ref[...] = d_h.astype(BF)
    d_gain_ref[...] = d_gain


def attention_back_kernel(me_ref, x_ref, gains_ref, cos_ref, sin_ref, d_low_ref, d_h_ref, q_ref, k_ref, v_ref, p0_ref, p1_ref, p2_ref, *refs):
    pieces, refs = refs[:6], refs[6:]
    (d_qkv_ref, grad_ref, d_gain_ref, w, d_o, d_q, d_k, d_v, sems) = refs
    copies = piece_copies(pieces, w, me_ref[0], ROWS, TOP, sems)
    for copy in copies:
        copy.start()
    for copy in copies:
        copy.wait()
    d_low = d_low_ref[...]
    for c in range(3):
        part = mult_nt(d_low, w[320 * c : 320 * (c + 1), :D]).astype(BF)
        for side in range(5):
            head = 5 * c + side
            for i in range(BLOCKS):
                at = i * STACK + head % GROUP * BLOCK
                d_o[head // GROUP, at : at + BLOCK, :] = part[i * BLOCK : (i + 1) * BLOCK, HEAD_DIM * side : HEAD_DIM * (side + 1)]
    probs = (p0_ref, p1_ref, p2_ref)

    def one_group(j, carry):
        parts_k, parts_v = [], []
        for i in range(BLOCKS):
            keys = (i + 1) * BLOCK
            stack = slice(i * STACK, (i + 1) * STACK)
            low = probs[i][j]
            d_one = d_o[j, stack, :]
            prob = low.astype(F32)
            d_prob = mult_nt(d_one, v_ref[j, :keys, :])
            inner = jnp.sum(prob * d_prob, axis=-1, keepdims=True)
            d_scores = (prob * (d_prob - inner)).astype(BF)
            d_q[j, stack, :] = mult(d_scores, k_ref[j, :keys, :]) * 0.125
            parts_k.append(mult_tn(d_scores, q_ref[j, stack, :]))
            parts_v.append(mult_tn(low, d_one))
        for i in range(BLOCKS):
            rows = slice(i * BLOCK, (i + 1) * BLOCK)
            d_k[j, rows, :] = sum(part[rows] for part in parts_k[i:]) * 0.125
            d_v[j, rows, :] = sum(part[rows] for part in parts_v[i:])
        return carry

    lax.fori_loop(0, KV, one_group, 0)
    for c in range(QK // 128):
        heads = []
        for head in (2 * c, 2 * c + 1):
            heads.append(stacked_head(d_q, head) if head < HEADS else d_k[head - HEADS])
        u = jnp.concatenate(heads, axis=1)
        d_qkv_ref[:, 128 * c : 128 * (c + 1)] = rope(u, cos_ref[...], sin_ref[...], -1.0).astype(BF)
    for c in range(3):
        heads = [d_v[j] for j in range(2 * c, min(2 * c + 2, KV))]
        wide = jnp.concatenate(heads, axis=1) if len(heads) > 1 else heads[0]
        d_qkv_ref[:, QK + 128 * c : QK + 128 * c + wide.shape[1]] = wide.astype(BF)
    d_a = mult_nt(d_qkv_ref[...], w[:, AT_QKV:])
    d_norm, d_gain = norm_back(x_ref[...].astype(F32), gains_ref[0:1], d_a)
    grad_ref[...] = d_h_ref[...] + d_norm
    d_gain_ref[...] = d_gain


FLIPS = (3, 2, 1, 0)


def down_grad_kernel(me_ref, act_ref, dy_ref, *outs):
    dy = dy_ref[...]
    for flip, out in zip(FLIPS, outs):
        at = pl.multiple_of(lax.bitwise_xor(me_ref[0], jnp.int32(flip)) * (FF // 4), 128)
        out[...] = mult_tn(act_ref[:, pl.ds(at, FF // 4)], dy).astype(BF)


def wide_grad_kernel(me_ref, b_ref, d_gate_ref, d_up_ref, *refs):
    outs, (full,) = refs[:4], refs[4:]
    for c in range(4):
        for k, source in enumerate((d_gate_ref, d_up_ref)):
            full[2 * c + k] = mult(b_ref[...], source[:, UNIT * c : UNIT * (c + 1)]).astype(BF)
            for flip, out in zip(FLIPS, outs):
                at = pl.multiple_of(lax.bitwise_xor(me_ref[0], jnp.int32(flip)) * ROWS, 16)
                out[c, ROWS * k : ROWS * (k + 1), :] = full[2 * c + k, pl.ds(at, ROWS), :]


def attention_grad_kernel(me_ref, a_ref, att_ref, d_qkv_ref, d_low_ref, gain_ref, *refs):
    outs, (full,) = refs[:4], refs[4:]
    a, att = a_ref[...], att_ref[...]
    full[0] = mult(a, d_qkv_ref[:, :UNIT]).astype(BF)
    full[1] = mult(a, d_qkv_ref[:, UNIT : 2 * UNIT]).astype(BF)
    full[2] = jnp.concatenate([mult(a, d_qkv_ref[:, 2 * UNIT :]), mult(att, d_low_ref[:, : UNIT // 2])], axis=1).astype(BF)
    full[3] = mult(att, d_low_ref[:, UNIT // 2 :]).astype(BF)
    for flip, out in zip(FLIPS, outs):
        place = lax.bitwise_xor(me_ref[0], jnp.int32(flip))
        at = pl.multiple_of(place * ROWS, 16)
        for c in range(4):
            out[c, :ROWS, :] = full[c, pl.ds(at, ROWS), :]
            out[c, ROWS:, :] = gain_ref[place] if c == 0 else jnp.zeros((16, UNIT), BF)


def final_kernel(place_ref, *refs):
    down, wide, first = refs[:4], refs[4:8], refs[8:12]
    (query_ref, key_ref, value_ref, proj_ref, gain_ref, gate_ref, up_ref, down_ref, full) = refs[12:]
    for k, by in enumerate((0, 3, 1, 2)):
        z = lax.rem(place_ref[0] + by, 4)
        x = lax.rem(place_ref[1] + by, 4)
        down_ref[pl.ds(pl.multiple_of(z * (FF // 16), 16), FF // 16), :] = down[k][...].astype(F32)
        columns = pl.ds(pl.multiple_of(x * UNIT, 128), UNIT)
        gate_ref[:, columns] = wide[k][:ROWS].astype(F32)
        up_ref[:, columns] = wide[k][ROWS:].astype(F32)
        full[:, pl.ds(pl.multiple_of(z * UNIT, 128), UNIT)] = first[k][...].astype(F32)
    query_ref[...] = full[:ROWS, :D]
    key_ref[...] = full[:ROWS, D:QK]
    value_ref[...] = full[:ROWS, QK:QKV]
    proj_ref[...] = full[:ROWS, QKV:]
    gain_ref[...] = full[ROWS : ROWS + 8, :256]


def run(kernel, name, ins, specs, outs, scratch, flops, out_specs=None):
    moved = sum(a.size * a.dtype.itemsize for a in ins) + sum(o.size * o.dtype.itemsize for o in outs)
    return pl.pallas_call(
        kernel,
        name=name,
        out_shape=outs,
        in_specs=specs,
        out_specs=out_specs or [VMEM] * len(outs),
        scratch_shapes=scratch,
        cost_estimate=pl.CostEstimate(flops=flops, bytes_accessed=moved, transcendentals=0),
        compiler_params=pltpu.CompilerParams(vmem_limit_bytes=LIMIT),
    )(*ins)


def swap_cores(value):
    return lax.ppermute(value, "core", [(0, 1), (1, 0)])


def shift_ring(value, axis, by):
    return lax.ppermute(value, axis, [(i, (i + by) % 4) for i in range(4)])


def shift_y(value, by):
    place = [(y % 2) * 2 + y // 2 for y in range(4)]
    return lax.ppermute(value, ("y_lo", "y_hi"), [(place[y], place[(y + by) % 4]) for y in range(4)])


def gathered(shard, top):
    near = swap_cores(shard)
    far = (shift_y(shard[:top], 1), shift_y(shard[top:], -1))
    return [shard, near, *far, swap_cores(far[0]), swap_cores(far[1])]


def in_order(parts, low, core):
    parts = jnp.where(core == 1, parts[jnp.array([1, 0, 3, 2])], parts)
    return jnp.where(low == 1, parts[jnp.array([2, 3, 0, 1])], parts)


def add_low(*terms):
    total = terms[0].astype(F32)
    for term in terms[1:]:
        total = total + term.astype(F32)
    return total.astype(BF)


def piece_of(value, axis, by):
    place = lax.rem(lax.axis_index(axis) + by, 4)
    return lax.dynamic_index_in_dim(value, place, 0, keepdims=False)


def ring_scatter(value, axis):
    got = [shift_ring(piece_of(value, axis, by % 4), axis, by) for by in (1, -1, 2)]
    return add_low(piece_of(value, axis, 0), *got)


def ring_gather(value, axis):
    return [value] + [shift_ring(value, axis, by) for by in (1, -1, 2)]


def ring_joined(value, axis):
    pieces = ring_gather(value, axis)
    out = jnp.zeros((4, *value.shape), value.dtype)
    place = lax.axis_index(axis)
    for by, piece in zip((0, 3, 1, 2), pieces):
        out = lax.dynamic_update_index_in_dim(out, piece, lax.rem(place + by, 4), 0)
    return out.reshape(4 * value.shape[0], *value.shape[1:])


def chip_pair(blocks):
    theirs = add_low(blocks[1], swap_cores(blocks[0]))
    mine = swap_cores(blocks[2])
    top, bottom = shift_y(theirs[:2], 1), shift_y(theirs[2:], -1)
    return add_low(blocks[3], mine, jnp.concatenate([top, bottom]))


def scattered(blocks, first, second):
    part = ring_scatter(chip_pair(blocks), first)
    part = ring_scatter(part.reshape(4, part.shape[0] // 4, part.shape[1]), second)
    return add_low(part, lax.ppermute(part, "y_hi", [(0, 1), (1, 0)]))


def body(tokens, lengths, norm_attn, w_query, w_key, w_value, w_out, norm_mlp, w_gate, w_up, w_down, cotangent):
    low, core = lax.axis_index("y_lo"), lax.axis_index("core")
    me = (low * 2 + core).astype(jnp.int32)[None]
    pad = jnp.zeros((ROWS, AT_QKV - D), BF)
    first = gathered(jnp.concatenate([w_out, pad, w_query, w_key, w_value], axis=1), TOP)
    own = jnp.stack([norm_attn, norm_mlp])
    pair = jnp.stack([own, shift_y(own, 1)])
    other = swap_cores(pair)
    gains = in_order(jnp.stack([pair[0], other[0], pair[1], other[1]]), low, core)
    gains = gains.transpose(1, 0, 2).reshape(2, D).astype(F32)
    wide = gathered(jnp.concatenate([w_gate, w_up], axis=1), TOP)
    down = gathered(w_down, FF // 8)

    x, dy = tokens[0], cotangent[0]
    slots = jnp.arange(T, dtype=jnp.int32)
    ends = jnp.cumsum(lengths[0])
    start = jnp.max(jnp.where(slots[:, None] >= ends[None, :], ends[None, :], 0), axis=1)
    freq = BASE ** (-jnp.arange(HEAD_DIM // 2, dtype=F32) * 2.0 / HEAD_DIM)
    angle = (slots - start).astype(F32)[:, None] * freq[None, :]
    cosine = jnp.tile(jnp.cos(angle), (1, 4))
    sine = jnp.sin(angle)
    sine = jnp.tile(jnp.concatenate([-sine, sine], axis=1), (1, 2))
    start = start[:, None]

    dma = pltpu.SemaphoreType.DMA
    a_low, q, k, v, p0, p1, p2, att, h, b_low = run(
        attention_kernel,
        "attention",
        (me, x, gains, cosine, sine, start, *first),
        [SMEM] + [VMEM] * 5 + [ANY] * 6,
        [
            shape(T, D),
            shape(KV, GROUP * T, HEAD_DIM),
            shape(KV, T, HEAD_DIM),
            shape(KV, T, HEAD_DIM),
            *(shape(KV, STACK, BLOCK * (i + 1)) for i in range(BLOCKS)),
            shape(T, D),
            shape(T, D, dtype=F32),
            shape(T, D),
        ],
        [pltpu.VMEM((D, PACK), BF), pltpu.VMEM((KV, GROUP * T, HEAD_DIM), F32), pltpu.VMEM((T, T), F32), dma((6,))],
        2 * T * D * 2560 + 4 * HEADS * T * T * 128,
    )
    act, silu, slope = run(
        gate_kernel,
        "gate_up",
        (me, b_low, *wide),
        [SMEM, VMEM] + [ANY] * 6,
        [shape(T, FF)] * 3,
        [pltpu.VMEM((D, 2 * FF), BF), dma((2 * FF // CHUNK, 6))],
        4 * T * D * FF,
    )
    down_blocks = run(
        down_grad_kernel,
        "down_grad",
        (me, act, dy),
        [SMEM, VMEM, VMEM],
        [shape(FF // 4, D)] * 4,
        [],
        2 * T * D * FF,
    )
    result, d_gate, d_up, d_h, d_low, d_gain_mlp = run(
        mlp_kernel,
        "mlp_back",
        (me, act, silu, slope, h, dy, gains, *down, *wide),
        [SMEM] + [VMEM] * 6 + [ANY] * 12,
        [shape(T, D), shape(T, FF), shape(T, FF), shape(T, D, dtype=F32), shape(T, D), shape(1, D, dtype=F32)],
        [pltpu.VMEM((FF, D), BF), pltpu.VMEM((D, 2 * FF), BF), pltpu.VMEM((T, D), F32), dma((2, 6))],
        8 * T * D * FF,
    )
    down_part = scattered([b.reshape(4, FF // 16, D) for b in down_blocks], "z", "x")
    wide_blocks = run(
        wide_grad_kernel,
        "gate_up_grad",
        (me, b_low.T, d_gate, d_up),
        [SMEM] + [VMEM] * 3,
        [shape(4, 2 * ROWS, UNIT)] * 4,
        [pltpu.VMEM((8, D, UNIT), BF)],
        4 * T * D * FF,
    )
    wide_part = scattered(wide_blocks, "x", "z")
    d_qkv, grad_input, d_gain_attn = run(
        attention_back_kernel,
        "attention_back",
        (me, x, gains, cosine, sine, d_low, d_h, q, k, v, p0, p1, p2, *first),
        [SMEM] + [VMEM] * 12 + [ANY] * 6,
        [shape(T, QKV), shape(T, D, dtype=F32), shape(1, D, dtype=F32)],
        [
            pltpu.VMEM((D, PACK), BF),
            pltpu.VMEM((KV, GROUP * T, HEAD_DIM), BF),
            pltpu.VMEM((KV, GROUP * T, HEAD_DIM), F32),
            pltpu.VMEM((KV, T, HEAD_DIM), F32),
            pltpu.VMEM((KV, T, HEAD_DIM), F32),
            dma((6,)),
        ],
        2 * T * D * 2560 + 8 * HEADS * T * T * 128,
    )
    d_gains = jnp.concatenate([d_gain_attn, d_gain_mlp]).reshape(2, 4, ROWS).transpose(1, 0, 2)
    d_gains = jnp.pad(d_gains, ((0, 0), (0, 14), (0, UNIT - ROWS))).astype(BF)
    first_blocks = run(
        attention_grad_kernel,
        "attention_grad",
        (me, a_low.T, att.T, d_qkv, d_low, d_gains),
        [SMEM] + [VMEM] * 5,
        [shape(4, ROWS + 16, UNIT)] * 4,
        [pltpu.VMEM((4, D, UNIT), BF)],
        2 * T * D * FF,
    )
    first_part = scattered(first_blocks, "z", "x")
    down_all = ring_gather(ring_joined(down_part, "x"), "z")
    wide_all = ring_gather(ring_joined(wide_part, "z"), "x")
    first_all = ring_gather(ring_joined(first_part, "x"), "z")
    place = jnp.stack([lax.axis_index("z"), lax.axis_index("x")]).astype(jnp.int32)
    query, key, value, proj, gain, gate, up, down_grad = run(
        final_kernel,
        "place_gradients",
        (place, *down_all, *wide_all, *first_all),
        [SMEM] + [VMEM] * 12,
        [
            shape(ROWS, D, dtype=F32),
            shape(ROWS, KV * HEAD_DIM, dtype=F32),
            shape(ROWS, KV * HEAD_DIM, dtype=F32),
            shape(ROWS, D, dtype=F32),
            shape(8, 256, dtype=F32),
            shape(ROWS, FF, dtype=F32),
            shape(ROWS, FF, dtype=F32),
            shape(FF // 4, D, dtype=F32),
        ],
        [pltpu.VMEM((ROWS + 16, FF), F32)],
        0,
    )
    return (result[None], grad_input[None], gain[0, :ROWS], query, key, value, proj, gain[1, :ROWS], gate, up, down_grad)


def solution(mesh):
    torus = Mesh(mesh.devices.reshape(2, 2, 4, 4, 2), EVERY)
    rows = P(EVERY, None, None)
    weight = P(SHARD, None)
    gain = P(SHARD)
    return jax.shard_map(
        body,
        mesh=torus,
        in_specs=(rows, P(EVERY, None), gain, weight, weight, weight, weight, gain, weight, weight, weight, rows),
        out_specs=(rows, rows, gain, weight, weight, weight, weight, gain, weight, weight, weight),
        check_vma=False,
    )
```

```python
import jax
import jax.numpy as jnp
from jax import lax
from jax.experimental import pallas as pl
from jax.experimental.pallas import tpu as pltpu
from jax.sharding import Mesh
from jax.sharding import PartitionSpec as P

T = 384
D = 960
FF = 2560
HEADS = 15
KV = 5
GROUP = 3
HEAD_DIM = 64
BLOCK = 128
BLOCKS = T // BLOCK
STACK = GROUP * BLOCK
QK = (HEADS + KV) * HEAD_DIM
QKV = QK + KV * HEAD_DIM
PACK = 2 * QK
ROWS = D // 4
UNIT = 640
EVERY = ("y_lo", "core", "z", "x", "y_hi")
SHARD = ("y_lo", "core")
EPS = 1e-05
BASE = 100000.0
MASKED = -1e30
BF = jnp.bfloat16
F32 = jnp.float32
LIMIT = 52 * 2**20

ANY = pl.BlockSpec(memory_space=pl.ANY)
VMEM = pl.BlockSpec(memory_space=pltpu.VMEM)
SMEM = pl.BlockSpec(memory_space=pltpu.SMEM)


def shape(*dims, dtype=BF):
    return jax.ShapeDtypeStruct(dims, dtype)


def mult(left, right):
    return jnp.dot(left, right, preferred_element_type=F32)


def mult_tn(left, right):
    return lax.dot_general(left, right, (((0,), (0,)), ((), ())), preferred_element_type=F32)


def mult_nt(left, right):
    return lax.dot_general(left, right, (((1,), (1,)), ((), ())), preferred_element_type=F32)


def shard_at(me, flip, rows, unit):
    return pl.ds(pl.multiple_of(lax.bitwise_xor(me, jnp.int32(flip)) * rows, unit), rows)


def row_copies(pieces, full, me, sems, columns=None, at=0):
    copies = []
    for flip, source in enumerate(pieces):
        width = source.shape[1]
        target = pl.ds(at, width)
        if columns is not None:
            source, target = source.at[:, columns], pl.ds(at + columns.start, columns.size)
        copies.append(pltpu.make_async_copy(source, full.at[shard_at(me, flip, ROWS, 16), target], sems.at[flip]))
    return copies


def column_copies(pieces, full, me, sems):
    copies = []
    for k, (flip, start, size) in enumerate(((0, 0, D), (1, 0, D), (2, 0, D // 2), (2, D // 2, D // 2), (3, 0, D // 2), (3, D // 2, D // 2))):
        target = full.at[pl.ds(start, size), shard_at(me, flip, FF // 4, 128)]
        copies.append(pltpu.make_async_copy(pieces[k], target, sems.at[k]))
    return copies


def start_all(copies):
    for copy in copies:
        copy.start()


def wait_all(copies):
    for copy in copies:
        copy.wait()


def rope(u, cosine, sine, sign):
    lane = lax.broadcasted_iota(jnp.int32, u.shape, 1)
    turned = jnp.where(lane % HEAD_DIM < HEAD_DIM // 2, pltpu.roll(u, 96, 1), pltpu.roll(u, 32, 1))
    return u * cosine + sign * (turned * sine)


def rms_scale(v):
    return lax.rsqrt(jnp.mean(v * v, axis=-1, keepdims=True) + EPS)


def norm_back(v, gain, grad):
    scale = rms_scale(v)
    inner = grad * gain
    d_v = scale * inner - v * (scale * scale * scale) * jnp.mean(v * inner, axis=-1, keepdims=True)
    return d_v, jnp.sum(grad * v * scale, axis=0, keepdims=True)


def attention_kernel(me_ref, x_ref, gains_ref, cos_ref, sin_ref, start_ref, *refs):
    pieces, refs = refs[:8], refs[8:]
    (a_ref, q_ref, k_ref, v_ref, p0_ref, p1_ref, p2_ref, att_ref, h_ref, b_ref, w, o, bias, sems) = refs
    copies = row_copies(pieces[:4], w, me_ref[0], sems.at[0])
    copies += row_copies(pieces[4:], w, me_ref[0], sems.at[1], at=QK)
    start_all(copies)
    x = x_ref[...].astype(F32)
    a_ref[...] = (x * rms_scale(x) * gains_ref[0:1]).astype(BF)
    column = lax.broadcasted_iota(jnp.int32, (T, T), 1)
    row = lax.broadcasted_iota(jnp.int32, (T, T), 0)
    bias[...] = jnp.where((column >= start_ref[...]) & (column <= row), 0.0, MASKED)
    wait_all(copies)
    a = a_ref[...]
    for c in range(QK // 256):
        wide = mult(a, w[:, 256 * c : 256 * (c + 1)])
        for half in range(2):
            u = rope(wide[:, 128 * half : 128 * half + 128], cos_ref[...], sin_ref[...], 1.0).astype(BF)
            for side in range(2):
                head = 4 * c + 2 * half + side
                one = u[:, HEAD_DIM * side : HEAD_DIM * (side + 1)]
                if head < HEADS:
                    for i in range(BLOCKS):
                        at = i * STACK + head % GROUP * BLOCK
                        q_ref[head // GROUP, at : at + BLOCK, :] = one[i * BLOCK : (i + 1) * BLOCK]
                else:
                    k_ref[head - HEADS] = one
    values = mult(a, w[:, QK + D :]).astype(BF)
    for j in range(KV):
        v_ref[j] = values[:, HEAD_DIM * j : HEAD_DIM * (j + 1)]
    probs = (p0_ref, p1_ref, p2_ref)

    def one_group(j, carry):
        for i in range(BLOCKS):
            keys = (i + 1) * BLOCK
            q = q_ref[j, i * STACK : (i + 1) * STACK, :]
            scores = mult_nt(q, k_ref[j, :keys, :]) * 0.125
            part = bias[i * BLOCK : (i + 1) * BLOCK, :keys]
            scores = scores + jnp.concatenate([part] * GROUP, axis=0)
            expo = jnp.exp(scores - jnp.max(scores, axis=-1, keepdims=True))
            prob = (expo * (1.0 / jnp.sum(expo, axis=-1, keepdims=True))).astype(BF)
            probs[i][j] = prob
            o[j, i * STACK : (i + 1) * STACK, :] = mult(prob, v_ref[j, :keys, :])
        return carry

    lax.fori_loop(0, KV, one_group, 0)
    for c in range(8):
        heads = [stacked_head(o, head) for head in range(2 * c, min(2 * c + 2, HEADS))]
        wide = jnp.concatenate(heads, axis=1) if len(heads) > 1 else heads[0]
        att_ref[:, 128 * c : 128 * c + wide.shape[1]] = wide.astype(BF)
    h = x_ref[...].astype(F32) + mult(att_ref[...], w[:, QK : QK + D])
    h_ref[...] = h
    b_ref[...] = (h * rms_scale(h) * gains_ref[1:2]).astype(BF)


def stacked_head(ref, head):
    at = head % GROUP * BLOCK
    return jnp.concatenate(
        [ref[head // GROUP, i * STACK + at : i * STACK + at + BLOCK, :] for i in range(BLOCKS)], axis=0
    )


CHUNK = 512


def gate_kernel(me_ref, b_ref, *refs):
    pieces, (act_ref, silu_ref, slope_ref, w, sems) = refs[:8], refs[8:]
    chunks = FF // CHUNK
    copies = []
    for c in range(chunks):
        for k in range(2):
            part = pieces[4 * k : 4 * k + 4]
            copies.append(row_copies(part, w, me_ref[0], sems.at[2 * c + k], pl.ds(c * CHUNK, CHUNK), k * FF))
    for group in copies:
        start_all(group)
    b = b_ref[...]
    for c in range(chunks):
        at = c * CHUNK
        for group in copies[2 * c : 2 * c + 2]:
            wait_all(group)
        gate = mult(b, w[:, at : at + CHUNK])
        up = mult(b, w[:, FF + at : FF + at + CHUNK])
        sigma = jax.nn.sigmoid(gate)
        silu = gate * sigma
        act_ref[:, at : at + CHUNK] = (silu * up).astype(BF)
        silu_ref[:, at : at + CHUNK] = silu.astype(BF)
        slope_ref[:, at : at + CHUNK] = (up * sigma * (1.0 + gate * (1.0 - sigma))).astype(BF)


def mlp_kernel(me_ref, act_ref, silu_ref, slope_ref, h_ref, dy_ref, gains_ref, *refs):
    down, wide, refs = refs[:6], refs[6:14], refs[15:]
    (out_ref, d_gate_ref, d_up_ref, d_h_ref, d_low_ref, d_gain_ref, wd, w, sums, sems) = refs
    first = column_copies(down, wd, me_ref[0], sems.at[0])
    second = row_copies(wide[:4], w, me_ref[0], sems.at[1]) + row_copies(wide[4:], w, me_ref[0], sems.at[2], at=FF)
    start_all(first + second)
    wait_all(first)
    dy = dy_ref[...]
    out_ref[...] = (h_ref[...] + mult_nt(act_ref[...], wd[...])).astype(BF)
    for c in range(FF // CHUNK):
        at = c * CHUNK
        d_act = mult(dy, wd[:, at : at + CHUNK])
        d_gate_ref[:, at : at + CHUNK] = (d_act * slope_ref[:, at : at + CHUNK].astype(F32)).astype(BF)
        d_up_ref[:, at : at + CHUNK] = (d_act * silu_ref[:, at : at + CHUNK].astype(F32)).astype(BF)
    wait_all(second)
    sums[...] = mult_nt(d_gate_ref[...], w[:, :FF]) + mult_nt(d_up_ref[...], w[:, FF:])
    d_norm, d_gain = norm_back(h_ref[...], gains_ref[1:2], sums[...])
    d_h = dy.astype(F32) + d_norm
    d_h_ref[...] = d_h
    d_low_ref[...] = d_h.astype(BF)
    d_gain_ref[...] = d_gain


def attention_back_kernel(me_ref, x_ref, gains_ref, cos_ref, sin_ref, d_low_ref, d_h_ref, q_ref, k_ref, v_ref, p0_ref, p1_ref, p2_ref, *refs):
    pieces, refs = refs[:8], refs[-9:]
    (d_qkv_ref, grad_ref, d_gain_ref, w, d_o, d_q, d_k, d_v, sems) = refs
    copies = row_copies(pieces[:4], w, me_ref[0], sems.at[0])
    copies += row_copies(pieces[4:], w, me_ref[0], sems.at[1], at=QK)
    start_all(copies)
    wait_all(copies)
    d_low = d_low_ref[...]
    for c in range(3):
        part = mult_nt(d_low, w[320 * c : 320 * (c + 1), QK : QK + D]).astype(BF)
        for side in range(5):
            head = 5 * c + side
            for i in range(BLOCKS):
                at = i * STACK + head % GROUP * BLOCK
                d_o[head // GROUP, at : at + BLOCK, :] = part[i * BLOCK : (i + 1) * BLOCK, HEAD_DIM * side : HEAD_DIM * (side + 1)]
    probs = (p0_ref, p1_ref, p2_ref)

    def one_group(j, carry):
        parts_k, parts_v = [], []
        for i in range(BLOCKS):
            keys = (i + 1) * BLOCK
            stack = slice(i * STACK, (i + 1) * STACK)
            low = probs[i][j]
            d_one = d_o[j, stack, :]
            prob = low.astype(F32)
            d_prob = mult_nt(d_one, v_ref[j, :keys, :])
            inner = jnp.sum(prob * d_prob, axis=-1, keepdims=True)
            d_scores = (prob * (d_prob - inner)).astype(BF)
            d_q[j, stack, :] = mult(d_scores, k_ref[j, :keys, :]) * 0.125
            parts_k.append(mult_tn(d_scores, q_ref[j, stack, :]))
            parts_v.append(mult_tn(low, d_one))
        for i in range(BLOCKS):
            rows = slice(i * BLOCK, (i + 1) * BLOCK)
            d_k[j, rows, :] = sum(part[rows] for part in parts_k[i:]) * 0.125
            d_v[j, rows, :] = sum(part[rows] for part in parts_v[i:])
        return carry

    lax.fori_loop(0, KV, one_group, 0)
    for c in range(QK // 128):
        heads = []
        for head in (2 * c, 2 * c + 1):
            heads.append(stacked_head(d_q, head) if head < HEADS else d_k[head - HEADS])
        u = jnp.concatenate(heads, axis=1)
        d_qkv_ref[:, 128 * c : 128 * (c + 1)] = rope(u, cos_ref[...], sin_ref[...], -1.0).astype(BF)
    for c in range(3):
        heads = [d_v[j] for j in range(2 * c, min(2 * c + 2, KV))]
        wide = jnp.concatenate(heads, axis=1) if len(heads) > 1 else heads[0]
        d_qkv_ref[:, QK + 128 * c : QK + 128 * c + wide.shape[1]] = wide.astype(BF)
    d_a = mult_nt(d_qkv_ref[:, :QK], w[:, :QK]) + mult_nt(d_qkv_ref[:, QK:], w[:, QK + D :])
    d_norm, d_gain = norm_back(x_ref[...].astype(F32), gains_ref[0:1], d_a)
    grad_ref[...] = d_h_ref[...] + d_norm
    d_gain_ref[...] = d_gain


FLIPS = (3, 1, 2, 0)


def down_grad_kernel(me_ref, dy_ref, act_ref, *refs):
    for flip, out in zip(FLIPS, refs[-4:]):
        part = act_ref[:, shard_at(me_ref[0], flip, FF // 4, 128)]
        for c in range(4):
            out[c, :ROWS, :] = mult(dy_ref[ROWS * c : ROWS * (c + 1), :], part).astype(BF)
            out[c, ROWS:, :] = jnp.zeros((16, UNIT), BF)


def wide_grad_kernel(me_ref, b_ref, d_gate_ref, d_up_ref, *refs):
    outs, full = refs[-5:-1], refs[-1]
    for k, source in enumerate((d_gate_ref, d_up_ref)):
        for c in range(4):
            full[4 * k + c] = mult(b_ref[...], source[:, UNIT * c : UNIT * (c + 1)]).astype(BF)
            for flip, out in zip(FLIPS, outs):
                out[k, c, :ROWS, :] = full[4 * k + c, shard_at(me_ref[0], flip, ROWS, 16), :]
                out[k, c, ROWS:, :] = jnp.zeros((16, UNIT), BF)


def attention_grad_kernel(me_ref, a_ref, att_ref, d_qkv_ref, d_low_ref, gain_ref, *refs):
    outs, full = refs[-5:-1], refs[-1]
    a, att = a_ref[...], att_ref[...]
    full[0] = mult(a, d_qkv_ref[:, :UNIT]).astype(BF)
    full[1] = mult(a, d_qkv_ref[:, UNIT : 2 * UNIT]).astype(BF)
    full[2] = jnp.concatenate([mult(a, d_qkv_ref[:, 2 * UNIT :]), mult(att, d_low_ref[:, : UNIT // 2])], axis=1).astype(BF)
    full[3] = mult(att, d_low_ref[:, UNIT // 2 :]).astype(BF)
    for flip, out in zip(FLIPS, outs):
        place = lax.bitwise_xor(me_ref[0], jnp.int32(flip))
        at = pl.multiple_of(place * ROWS, 16)
        for c in range(4):
            out[c, :ROWS, :] = full[c, pl.ds(at, ROWS), :]
            out[c, ROWS:, :] = gain_ref[place] if c == 0 else jnp.zeros((16, UNIT), BF)


def place_all(first_place, second_place, pieces, full):
    size = full.shape[0] // 4
    for k, by in enumerate((0, 3, 1, 2)):
        columns = pl.ds(pl.multiple_of(lax.rem(first_place + by, 4) * UNIT, 128), UNIT)
        for j, other in enumerate((0, 3, 1, 2)):
            rows = pl.ds(pl.multiple_of(lax.rem(second_place + other, 4) * size, 16), size)
            if k < 3:
                part = pieces[k][size * j : size * (j + 1), :]
            else:
                at = size * (j % 2)
                part = pieces[3 + j // 2][at : at + size, :]
            full[rows, columns] = part.astype(F32)


def place_left_kernel(place_ref, *refs):
    pieces, (gate_ref, query_ref, key_ref, value_ref, proj_ref, gain_ref, full) = refs[:5], refs[5:]
    place_all(place_ref[0], place_ref[1], pieces, full)
    rows = slice(ROWS + 16, 2 * ROWS + 16)
    gate_ref[...] = full[:ROWS, :]
    query_ref[...] = full[rows, :D]
    key_ref[...] = full[rows, D:QK].T
    value_ref[...] = full[rows, QK:QKV].T
    proj_ref[...] = full[rows, QKV:]
    gain_ref[...] = full[2 * ROWS + 16 : 2 * ROWS + 24, :256]


def place_right_kernel(place_ref, *refs):
    pieces, (up_ref, down_ref, full) = refs[:5], refs[5:]
    place_all(place_ref[1], place_ref[0], pieces, full)
    up_ref[...] = full[:ROWS, :]
    for c in range(4):
        down_ref[ROWS * c : ROWS * (c + 1), :] = full[ROWS + 16 : 2 * ROWS + 16, UNIT * c : UNIT * (c + 1)]


def run(kernel, name, ins, specs, outs, scratch, flops, out_specs=None):
    moved = sum(a.size * a.dtype.itemsize for a in ins) + sum(o.size * o.dtype.itemsize for o in outs)
    return pl.pallas_call(
        kernel,
        name=name,
        out_shape=outs,
        in_specs=specs,
        out_specs=out_specs or [VMEM] * len(outs),
        scratch_shapes=scratch,
        cost_estimate=pl.CostEstimate(flops=flops, bytes_accessed=moved, transcendentals=0),
        compiler_params=pltpu.CompilerParams(vmem_limit_bytes=LIMIT),
    )(*ins)


def swap_cores(value):
    return lax.ppermute(value, "core", [(0, 1), (1, 0)])


def shift_y(value, by):
    place = [(y % 2) * 2 + y // 2 for y in range(4)]
    return lax.ppermute(value, ("y_lo", "y_hi"), [(place[y], place[(y + by) % 4]) for y in range(4)])


def in_order(parts):
    core = lax.axis_index("core") == 1
    low = lax.axis_index("y_lo") == 1
    near = [jnp.where(core, parts[k ^ 1], parts[k]) for k in range(4)]
    return jnp.stack([jnp.where(low, near[k ^ 2], near[k]) for k in range(4)])


def after(value, *others):
    return lax.optimization_barrier((value, *others))[0]


def add_low(*terms):
    total = terms[0].astype(F32)
    for term in terms[1:]:
        total = total + term.astype(F32)
    return total.astype(BF)


def shift_ring(value, axis, by):
    return lax.ppermute(value, axis, [(i, (i + by) % 4) for i in range(4)])


def halves(value):
    half = value.shape[0] // 2
    return value[:half], value[half:]


def ring_scatter(*parts):
    sent = []
    for value, axis in parts:
        place = lax.axis_index(axis)
        own, before, behind, across = [
            lax.dynamic_index_in_dim(value, lax.rem(place + by, 4), 0, keepdims=False) for by in (0, 3, 1, 2)
        ]
        top, bottom = halves(across)
        sent.append((axis, own, before, behind, shift_ring(top, axis, 1), shift_ring(bottom, axis, -1)))
    moved = []
    for axis, own, before, behind, top, bottom in sent:
        behind = jnp.concatenate([add_low(halves(behind)[0], top), halves(behind)[1]])
        before = jnp.concatenate([halves(before)[0], add_low(halves(before)[1], bottom)])
        moved.append((own, shift_ring(behind, axis, 1), shift_ring(before, axis, -1)))
    return [add_low(*terms) for terms in moved]


def ring_gather(*parts):
    first = [(value, axis, shift_ring(value, axis, 1), shift_ring(value, axis, -1)) for value, axis in parts]
    return [
        [value, before, behind, shift_ring(halves(before)[0], axis, 1), shift_ring(halves(behind)[1], axis, -1)]
        for value, axis, before, behind in first
    ]


def body(tokens, lengths, norm_attn, w_query, w_key, w_value, w_out, norm_mlp, w_gate, w_up, w_down, cotangent):
    low, core = lax.axis_index("y_lo"), lax.axis_index("core")
    me = (low * 2 + core).astype(jnp.int32)[None]
    first = [jnp.concatenate([w_query, w_key], axis=1), jnp.concatenate([w_out, w_value], axis=1)]
    far = [shift_y(first[0], 1), shift_y(first[1], -1)]
    near = [swap_cores(m) for m in first]
    own_gains = jnp.stack([norm_attn, norm_mlp])
    far_gains = shift_y(own_gains, 1)
    pair = jnp.stack([own_gains, far_gains])
    other = swap_cores(pair)
    gains = in_order([pair[0], other[0], pair[1], other[1]]).transpose(1, 0, 2).reshape(2, D).astype(F32)
    first = [piece for k in range(2) for piece in (first[k], near[k], far[k], swap_cores(far[k]))]
    x, dy = tokens[0], cotangent[0]
    near_wide = swap_cores(w_gate), swap_cores(w_up)
    near_down = swap_cores(w_down.T)
    held_gate, held_up, x, dy = lax.optimization_barrier((w_gate, w_up, x, dy, *far, other, near_down, *near_wide))[:4]
    far_gate, far_up = shift_y(held_gate, 1), shift_y(held_up, -1)
    held_down = after(w_down.T, far_gate, far_up)
    far_down = (shift_y(held_down[: D // 2], 1), shift_y(held_down[D // 2 :], -1))

    slots = jnp.arange(T, dtype=jnp.int32)
    ends = jnp.cumsum(lengths[0])
    start = jnp.max(jnp.where(slots[:, None] >= ends[None, :], ends[None, :], 0), axis=1)
    freq = BASE ** (-jnp.arange(HEAD_DIM // 2, dtype=F32) * 2.0 / HEAD_DIM)
    angle = (slots - start).astype(F32)[:, None] * freq[None, :]
    cosine = jnp.tile(jnp.cos(angle), (1, 4))
    sine = jnp.sin(angle)
    sine = jnp.tile(jnp.concatenate([-sine, sine], axis=1), (1, 2))
    start = start[:, None]

    dma = pltpu.SemaphoreType.DMA
    a_low, q, k, v, p0, p1, p2, att, h, b_low = run(
        attention_kernel,
        "attention",
        (me, x, gains, cosine, sine, start, *first),
        [SMEM] + [VMEM] * 5 + [ANY] * 8,
        [
            shape(T, D),
            shape(KV, GROUP * T, HEAD_DIM),
            shape(KV, T, HEAD_DIM),
            shape(KV, T, HEAD_DIM),
            *(shape(KV, STACK, BLOCK * (i + 1)) for i in range(BLOCKS)),
            shape(T, D),
            shape(T, D, dtype=F32),
            shape(T, D),
        ],
        [pltpu.VMEM((D, PACK), BF), pltpu.VMEM((KV, GROUP * T, HEAD_DIM), F32), pltpu.VMEM((T, T), F32), dma((2, 4))],
        2 * T * D * 2560 + 4 * HEADS * T * T * 128,
    )
    held = [swap_cores(after(part, b_low)) for part in (far_gate, far_up)]
    wide = [w_gate, near_wide[0], far_gate, held[0], w_up, near_wide[1], far_up, held[1]]
    act, silu, slope = run(
        gate_kernel,
        "gate_up",
        (me, b_low, *wide),
        [SMEM, VMEM] + [ANY] * 8,
        [shape(T, FF)] * 3,
        [pltpu.VMEM((D, 2 * FF), BF), dma((2 * FF // CHUNK, 4))],
        4 * T * D * FF,
    )
    down = [w_down.T, near_down, *far_down, *(swap_cores(after(part, act)) for part in far_down)]
    down_blocks = run(
        down_grad_kernel,
        "down_grad",
        (me, cotangent[0].T, act, *far_down),
        [SMEM, VMEM, VMEM, ANY, ANY],
        [shape(4, ROWS + 16, UNIT)] * 4,
        [],
        2 * T * D * FF,
    )
    down_got = [swap_cores(down_blocks[k]) for k in range(2)]
    result, d_gate, d_up, d_h, d_low, d_gain_mlp = run(
        mlp_kernel,
        "mlp_back",
        (me, act, silu, slope, h, dy, gains, *down, *wide, down_blocks[0]),
        [SMEM] + [VMEM] * 6 + [ANY] * 15,
        [shape(T, D), shape(T, FF), shape(T, FF), shape(T, D, dtype=F32), shape(T, D), shape(1, D, dtype=F32)],
        [pltpu.VMEM((D, FF), BF), pltpu.VMEM((D, 2 * FF), BF), pltpu.VMEM((T, D), F32), dma((3, 6))],
        8 * T * D * FF,
    )
    down_theirs = [add_low(down_blocks[2][part], down_got[0][part]) for part in (slice(0, 2), slice(2, 4))]
    down_y = [shift_y(down_theirs[0], 1), shift_y(down_theirs[1], -1)]
    wide_blocks = run(
        wide_grad_kernel,
        "gate_up_grad",
        (me, b_low.T, d_gate, d_up, *down_theirs),
        [SMEM] + [VMEM] * 3 + [ANY] * 2,
        [shape(2, 4, ROWS + 16, UNIT)] * 4,
        [pltpu.VMEM((8, D, UNIT), BF)],
        4 * T * D * FF,
    )
    wide_got = [swap_cores(wide_blocks[k]) for k in range(2)]
    wide_theirs = [add_low(wide_blocks[2][k], wide_got[0][k]) for k in range(2)]
    wide_y = [shift_y(wide_theirs[0], 1), shift_y(wide_theirs[1], -1)]
    d_qkv, grad_input, d_gain_attn = run(
        attention_back_kernel,
        "attention_back",
        (me, x, gains, cosine, sine, d_low, d_h, q, k, v, p0, p1, p2, *first, *wide_theirs, *down_y),
        [SMEM] + [VMEM] * 12 + [ANY] * 12,
        [shape(T, QKV), shape(T, D, dtype=F32), shape(1, D, dtype=F32)],
        [
            pltpu.VMEM((D, PACK), BF),
            pltpu.VMEM((KV, GROUP * T, HEAD_DIM), BF),
            pltpu.VMEM((KV, GROUP * T, HEAD_DIM), F32),
            pltpu.VMEM((KV, T, HEAD_DIM), F32),
            pltpu.VMEM((KV, T, HEAD_DIM), F32),
            dma((2, 4)),
        ],
        2 * T * D * 2560 + 8 * HEADS * T * T * 128,
    )
    d_gains = jnp.concatenate([d_gain_attn, d_gain_mlp]).reshape(2, 4, ROWS).transpose(1, 0, 2)
    d_gains = jnp.pad(d_gains, ((0, 0), (0, 14), (0, UNIT - ROWS))).astype(BF)
    first_blocks = run(
        attention_grad_kernel,
        "attention_grad",
        (me, a_low.T, att.T, d_qkv, d_low, d_gains, *wide_y),
        [SMEM] + [VMEM] * 5 + [ANY] * 2,
        [shape(4, ROWS + 16, UNIT)] * 4,
        [pltpu.VMEM((4, D, UNIT), BF)],
        2 * T * D * FF,
    )
    first_got = [swap_cores(first_blocks[k]) for k in range(2)]
    first_theirs = [add_low(first_blocks[2][part], first_got[0][part]) for part in (slice(0, 2), slice(2, 4))]
    first_y = [shift_y(first_theirs[0], 1), shift_y(first_theirs[1], -1)]
    sum_gate, sum_up = [add_low(wide_blocks[3][k], wide_got[1][k], wide_y[k]) for k in range(2)]
    sum_down = add_low(down_blocks[3], down_got[1], jnp.concatenate(down_y))
    sum_first = add_low(first_blocks[3], first_got[1], jnp.concatenate(first_y))
    result, grad_input, sum_first = lax.optimization_barrier((result.T, grad_input.T, sum_first))
    left = jnp.concatenate([sum_gate, sum_first], axis=1)
    right = jnp.concatenate([sum_up, sum_down], axis=1)
    left, right = ring_scatter((left, "z"), (right, "x"))
    left, right = ring_scatter((left.reshape(4, -1, UNIT), "x"), (right.reshape(4, -1, UNIT), "z"))
    both = jnp.stack([left, right])
    left, right = add_low(both, lax.ppermute(both, "y_hi", [(0, 1), (1, 0)]))
    left, right = ring_gather((left, "x"), (right, "z"))
    left, right = ring_gather((jnp.concatenate(left), "z"), (jnp.concatenate(right), "x"))

    places = jnp.stack([lax.axis_index("z"), lax.axis_index("x")]).astype(jnp.int32)
    specs = [SMEM] + [VMEM] * 5
    up, down_grad = run(
        place_right_kernel,
        "place_up_down",
        (places, *right),
        specs,
        [shape(ROWS, FF, dtype=F32), shape(D, UNIT, dtype=F32)],
        [pltpu.VMEM((2 * (ROWS + 16), FF), F32)],
        0,
    )
    gate, query, key, value, proj, gain = run(
        place_left_kernel,
        "place_gate_attention",
        (places, *left),
        specs,
        [
            shape(ROWS, FF, dtype=F32),
            shape(ROWS, D, dtype=F32),
            shape(KV * HEAD_DIM, ROWS, dtype=F32),
            shape(KV * HEAD_DIM, ROWS, dtype=F32),
            shape(ROWS, D, dtype=F32),
            shape(8, 256, dtype=F32),
        ],
        [pltpu.VMEM((2 * (ROWS + 16), FF), F32)],
        0,
    )
    down_grad = down_grad.T
    return (result.T[None], grad_input.T[None], gain[0, :ROWS], query, key.T, value.T, proj, gain[1, :ROWS], gate, up, down_grad)


def solution(mesh):
    torus = Mesh(mesh.devices.reshape(2, 2, 4, 4, 2), EVERY)
    rows = P(EVERY, None, None)
    weight = P(SHARD, None)
    gain = P(SHARD)
    return jax.shard_map(
        body,
        mesh=torus,
        in_specs=(rows, P(EVERY, None), gain, weight, weight, weight, weight, gain, weight, weight, weight, rows),
        out_specs=(rows, rows, gain, weight, weight, weight, weight, gain, weight, weight, weight),
        check_vma=False,
    )
```

```python
import jax
import jax.numpy as jnp
from jax import lax
from jax.experimental import pallas as pl
from jax.experimental.pallas import tpu as pltpu
from jax.sharding import Mesh
from jax.sharding import PartitionSpec as P

T = 384
D = 960
FF = 2560
HEADS = 15
KV = 5
GROUP = 3
HEAD_DIM = 64
BLOCK = 128
BLOCKS = T // BLOCK
STACK = GROUP * BLOCK
QK = (HEADS + KV) * HEAD_DIM
QKV = QK + KV * HEAD_DIM
PACK = 2 * QK
ROWS = D // 4
UNIT = 640
EVERY = ("y_lo", "core", "z", "x", "y_hi")
SHARD = ("y_lo", "core")
EPS = 1e-05
BASE = 100000.0
MASKED = -1e30
BF = jnp.bfloat16
F32 = jnp.float32
LIMIT = 52 * 2**20

ANY = pl.BlockSpec(memory_space=pl.ANY)
VMEM = pl.BlockSpec(memory_space=pltpu.VMEM)
SMEM = pl.BlockSpec(memory_space=pltpu.SMEM)


def shape(*dims, dtype=BF):
    return jax.ShapeDtypeStruct(dims, dtype)


def mult(left, right):
    return jnp.dot(left, right, preferred_element_type=F32)


def mult_tn(left, right):
    return lax.dot_general(left, right, (((0,), (0,)), ((), ())), preferred_element_type=F32)


def mult_nt(left, right):
    return lax.dot_general(left, right, (((1,), (1,)), ((), ())), preferred_element_type=F32)


def shard_at(me, flip, rows, unit):
    return pl.ds(pl.multiple_of(lax.bitwise_xor(me, jnp.int32(flip)) * rows, unit), rows)


def row_copies(pieces, full, me, sems, columns=None, at=0):
    copies = []
    for flip, source in enumerate(pieces):
        width = source.shape[1]
        target = pl.ds(at, width)
        if columns is not None:
            source, target = source.at[:, columns], pl.ds(at + columns.start, columns.size)
        copies.append(pltpu.make_async_copy(source, full.at[shard_at(me, flip, ROWS, 16), target], sems.at[flip]))
    return copies


def column_copies(pieces, full, me, sems):
    copies = []
    for k, (flip, start, size) in enumerate(((0, 0, D), (1, 0, D), (2, 0, D // 2), (2, D // 2, D // 2), (3, 0, D // 2), (3, D // 2, D // 2))):
        target = full.at[pl.ds(start, size), shard_at(me, flip, FF // 4, 128)]
        copies.append(pltpu.make_async_copy(pieces[k], target, sems.at[k]))
    return copies


def start_all(copies):
    for copy in copies:
        copy.start()


def wait_all(copies):
    for copy in copies:
        copy.wait()


def rope(u, cosine, sine, sign):
    lane = lax.broadcasted_iota(jnp.int32, u.shape, 1)
    turned = jnp.where(lane % HEAD_DIM < HEAD_DIM // 2, pltpu.roll(u, 96, 1), pltpu.roll(u, 32, 1))
    return u * cosine + sign * (turned * sine)


def rms_scale(v):
    return lax.rsqrt(jnp.mean(v * v, axis=-1, keepdims=True) + EPS)


def norm_back(v, gain, grad):
    scale = rms_scale(v)
    inner = grad * gain
    d_v = scale * inner - v * (scale * scale * scale) * jnp.mean(v * inner, axis=-1, keepdims=True)
    return d_v, jnp.sum(grad * v * scale, axis=0, keepdims=True)


def attention_kernel(me_ref, x_ref, gains_ref, cos_ref, sin_ref, start_ref, *refs):
    pieces, refs = refs[:8], refs[8:]
    (q_ref, k_ref, v_ref, p0_ref, p1_ref, p2_ref, x_out_ref, h_ref, b_ref, a_turned_ref, att_turned_ref, b_turned_ref, w, o, bias, att_ref, sems) = refs
    copies = row_copies(pieces[:4], w, me_ref[0], sems.at[0])
    copies += row_copies(pieces[4:], w, me_ref[0], sems.at[1], at=QK)
    start_all(copies)
    x_out_ref[...] = x_ref[...].T
    x = x_out_ref[...].astype(F32)
    a = (x * rms_scale(x) * gains_ref[0:1]).astype(BF)
    a_turned_ref[...] = a.T
    column = lax.broadcasted_iota(jnp.int32, (T, T), 1)
    row = lax.broadcasted_iota(jnp.int32, (T, T), 0)
    bias[...] = jnp.where((column >= start_ref[...]) & (column <= row), 0.0, MASKED)
    wait_all(copies)
    for c in range(QK // 256):
        wide = mult(a, w[:, 256 * c : 256 * (c + 1)])
        for half in range(2):
            u = rope(wide[:, 128 * half : 128 * half + 128], cos_ref[...], sin_ref[...], 1.0).astype(BF)
            for side in range(2):
                head = 4 * c + 2 * half + side
                one = u[:, HEAD_DIM * side : HEAD_DIM * (side + 1)]
                if head < HEADS:
                    for i in range(BLOCKS):
                        at = i * STACK + head % GROUP * BLOCK
                        q_ref[head // GROUP, at : at + BLOCK, :] = one[i * BLOCK : (i + 1) * BLOCK]
                else:
                    k_ref[head - HEADS] = one
    values = mult(a, w[:, QK + D :]).astype(BF)
    for j in range(KV):
        v_ref[j] = values[:, HEAD_DIM * j : HEAD_DIM * (j + 1)]
    probs = (p0_ref, p1_ref, p2_ref)

    def one_group(j, carry):
        for i in range(BLOCKS):
            keys = (i + 1) * BLOCK
            q = q_ref[j, i * STACK : (i + 1) * STACK, :]
            scores = mult_nt(q, k_ref[j, :keys, :]) * 0.125
            part = bias[i * BLOCK : (i + 1) * BLOCK, :keys]
            scores = scores + jnp.concatenate([part] * GROUP, axis=0)
            expo = jnp.exp(scores - jnp.max(scores, axis=-1, keepdims=True))
            prob = (expo * (1.0 / jnp.sum(expo, axis=-1, keepdims=True))).astype(BF)
            probs[i][j] = prob
            o[j, i * STACK : (i + 1) * STACK, :] = mult(prob, v_ref[j, :keys, :])
        return carry

    lax.fori_loop(0, KV, one_group, 0, unroll=True)
    for c in range(8):
        heads = [stacked_head(o, head) for head in range(2 * c, min(2 * c + 2, HEADS))]
        wide = jnp.concatenate(heads, axis=1) if len(heads) > 1 else heads[0]
        att_ref[:, 128 * c : 128 * c + wide.shape[1]] = wide.astype(BF)
    att = att_ref[...]
    att_turned_ref[...] = att.T
    h = x_out_ref[...].astype(F32) + mult(att, w[:, QK : QK + D])
    h_ref[...] = h
    b = (h * rms_scale(h) * gains_ref[1:2]).astype(BF)
    b_ref[...] = b
    b_turned_ref[...] = b.T


def stacked_head(ref, head):
    at = head % GROUP * BLOCK
    return jnp.concatenate(
        [ref[head // GROUP, i * STACK + at : i * STACK + at + BLOCK, :] for i in range(BLOCKS)], axis=0
    )


CHUNK = 512


def gate_kernel(me_ref, b_ref, *refs):
    pieces, (act_ref, silu_ref, slope_ref, w, sems) = refs[:8], refs[8:]
    chunks = FF // CHUNK
    copies = []
    for c in range(chunks):
        for k in range(2):
            part = pieces[4 * k : 4 * k + 4]
            copies.append(row_copies(part, w, me_ref[0], sems.at[2 * c + k], pl.ds(c * CHUNK, CHUNK), k * FF))
    for group in copies:
        start_all(group)
    b = b_ref[...]
    for c in range(chunks):
        at = c * CHUNK
        for group in copies[2 * c : 2 * c + 2]:
            wait_all(group)
        gate = mult(b, w[:, at : at + CHUNK])
        up = mult(b, w[:, FF + at : FF + at + CHUNK])
        sigma = jax.nn.sigmoid(gate)
        silu = gate * sigma
        act_ref[:, at : at + CHUNK] = (silu * up).astype(BF)
        silu_ref[:, at : at + CHUNK] = silu.astype(BF)
        slope_ref[:, at : at + CHUNK] = (up * sigma * (1.0 + gate * (1.0 - sigma))).astype(BF)


def mlp_kernel(me_ref, act_ref, silu_ref, slope_ref, h_ref, dy_ref, gains_ref, *refs):
    down, wide, refs = refs[:6], refs[6:14], refs[16:]
    (out_ref, d_gate_ref, d_up_ref, d_h_ref, d_low_ref, d_gain_ref, wd, w, sums, sems) = refs
    first = column_copies(down, wd, me_ref[0], sems.at[0])
    second = row_copies(wide[:4], w, me_ref[0], sems.at[1]) + row_copies(wide[4:], w, me_ref[0], sems.at[2], at=FF)
    start_all(first + second)
    wait_all(first)
    dy = dy_ref[...].T
    out_ref[...] = (h_ref[...] + mult_nt(act_ref[...], wd[...])).astype(BF)
    for c in range(FF // CHUNK):
        at = c * CHUNK
        d_act = mult(dy, wd[:, at : at + CHUNK])
        d_gate_ref[:, at : at + CHUNK] = (d_act * slope_ref[:, at : at + CHUNK].astype(F32)).astype(BF)
        d_up_ref[:, at : at + CHUNK] = (d_act * silu_ref[:, at : at + CHUNK].astype(F32)).astype(BF)
    wait_all(second)
    sums[...] = mult_nt(d_gate_ref[...], w[:, :FF]) + mult_nt(d_up_ref[...], w[:, FF:])
    d_norm, d_gain = norm_back(h_ref[...], gains_ref[1:2], sums[...])
    d_h = dy.astype(F32) + d_norm
    d_h_ref[...] = d_h
    d_low_ref[...] = d_h.astype(BF)
    d_gain_ref[...] = d_gain


def attention_back_kernel(me_ref, x_ref, gains_ref, cos_ref, sin_ref, d_low_ref, d_h_ref, q_ref, k_ref, v_ref, p0_ref, p1_ref, p2_ref, *refs):
    pieces, refs = refs[:8], refs[-9:]
    (d_qkv_ref, grad_ref, d_gain_ref, w, d_o, d_q, d_k, d_v, sems) = refs
    copies = row_copies(pieces[:4], w, me_ref[0], sems.at[0])
    copies += row_copies(pieces[4:], w, me_ref[0], sems.at[1], at=QK)
    start_all(copies)
    wait_all(copies)
    d_low = d_low_ref[...]
    for c in range(3):
        part = mult_nt(d_low, w[320 * c : 320 * (c + 1), QK : QK + D]).astype(BF)
        for side in range(5):
            head = 5 * c + side
            for i in range(BLOCKS):
                at = i * STACK + head % GROUP * BLOCK
                d_o[head // GROUP, at : at + BLOCK, :] = part[i * BLOCK : (i + 1) * BLOCK, HEAD_DIM * side : HEAD_DIM * (side + 1)]
    probs = (p0_ref, p1_ref, p2_ref)

    def one_group(j, carry):
        parts_k, parts_v = [], []
        for i in range(BLOCKS):
            keys = (i + 1) * BLOCK
            stack = slice(i * STACK, (i + 1) * STACK)
            low = probs[i][j]
            d_one = d_o[j, stack, :]
            prob = low.astype(F32)
            d_prob = mult_nt(d_one, v_ref[j, :keys, :])
            inner = jnp.sum(prob * d_prob, axis=-1, keepdims=True)
            d_scores = (prob * (d_prob - inner)).astype(BF)
            d_q[j, stack, :] = mult(d_scores, k_ref[j, :keys, :]) * 0.125
            parts_k.append(mult_tn(d_scores, q_ref[j, stack, :]))
            parts_v.append(mult_tn(low, d_one))
        for i in range(BLOCKS):
            rows = slice(i * BLOCK, (i + 1) * BLOCK)
            d_k[j, rows, :] = sum(part[rows] for part in parts_k[i:]) * 0.125
            d_v[j, rows, :] = sum(part[rows] for part in parts_v[i:])
        return carry

    lax.fori_loop(0, KV, one_group, 0, unroll=True)
    for c in range(QK // 128):
        heads = []
        for head in (2 * c, 2 * c + 1):
            heads.append(stacked_head(d_q, head) if head < HEADS else d_k[head - HEADS])
        u = jnp.concatenate(heads, axis=1)
        d_qkv_ref[:, 128 * c : 128 * (c + 1)] = rope(u, cos_ref[...], sin_ref[...], -1.0).astype(BF)
    for c in range(3):
        heads = [d_v[j] for j in range(2 * c, min(2 * c + 2, KV))]
        wide = jnp.concatenate(heads, axis=1) if len(heads) > 1 else heads[0]
        d_qkv_ref[:, QK + 128 * c : QK + 128 * c + wide.shape[1]] = wide.astype(BF)
    d_a = mult_nt(d_qkv_ref[:, :QK], w[:, :QK]) + mult_nt(d_qkv_ref[:, QK:], w[:, QK + D :])
    d_norm, d_gain = norm_back(x_ref[...].astype(F32), gains_ref[0:1], d_a)
    grad_ref[...] = d_h_ref[...] + d_norm
    d_gain_ref[...] = d_gain


FLIPS = (3, 1, 2, 0)


def block_copies(full, outs, sems, me, chunk):
    return [
        pltpu.make_async_copy(full.at[chunk, shard_at(me, flip, ROWS, 16)], out.at[chunk, pl.ds(0, ROWS)], sems.at[chunk, k])
        for k, (flip, out) in enumerate(zip(FLIPS, outs))
    ]


def down_grad_kernel(me_ref, dy_ref, act_ref, *refs):
    outs, full, sems = refs[-6:-2], refs[-2], refs[-1]
    copies = []
    for k, (flip, out) in enumerate(zip(FLIPS, outs)):
        part = act_ref[:, shard_at(me_ref[0], flip, FF // 4, 128)]
        for c in range(4):
            full[k, c] = mult(dy_ref[ROWS * c : ROWS * (c + 1), :], part).astype(BF)
            copies.append(pltpu.make_async_copy(full.at[k, c], out.at[c, pl.ds(0, ROWS)], sems.at[k, c]))
            copies[-1].start()
    wait_all(copies)


def wide_grad_kernel(me_ref, b_ref, d_ref, *refs):
    outs, full, sems = refs[-6:-2], refs[-2], refs[-1]
    copies = []
    for c in range(4):
        full[c] = mult(b_ref[...], d_ref[:, UNIT * c : UNIT * (c + 1)]).astype(BF)
        copies += block_copies(full, outs, sems, me_ref[0], c)
        start_all(copies[-4:])
    wait_all(copies)


def attention_grad_kernel(me_ref, a_ref, att_ref, d_qkv_ref, d_low_ref, gain_ref, *refs):
    outs, full, sems, gain_sems = refs[-7:-3], refs[-3], refs[-2], refs[-1]
    a, att = a_ref[...], att_ref[...]
    copies = []
    for k, (flip, out) in enumerate(zip(FLIPS, outs)):
        place = lax.bitwise_xor(me_ref[0], jnp.int32(flip))
        copies.append(pltpu.make_async_copy(gain_ref.at[place], out.at[0, pl.ds(ROWS, 16)], gain_sems.at[k]))
    start_all(copies)
    for c in range(4):
        if c < 2:
            block = mult(a, d_qkv_ref[:, UNIT * c : UNIT * (c + 1)])
        elif c == 2:
            block = jnp.concatenate([mult(a, d_qkv_ref[:, 2 * UNIT :]), mult(att, d_low_ref[:, : UNIT // 2])], axis=1)
        else:
            block = mult(att, d_low_ref[:, UNIT // 2 :])
        full[c] = block.astype(BF)
        copies += block_copies(full, outs, sems, me_ref[0], c)
        start_all(copies[-4:])
    wait_all(copies)


def place_all(first_place, second_place, pieces, full, done):
    size = full.shape[0] // 4
    for k, by in enumerate((0, 3, 1, 2)):
        place = lax.rem(first_place + by, 4)
        columns = pl.ds(pl.multiple_of(place * UNIT, 128), UNIT)
        for j, other in enumerate((0, 3, 1, 2)):
            rows = pl.ds(pl.multiple_of(lax.rem(second_place + other, 4) * size, 16), size)
            if k < 3:
                part = pieces[k][size * j : size * (j + 1), :]
            else:
                at = size * (j % 2)
                part = pieces[3 + j // 2][at : at + size, :]
            full[rows, columns] = part.astype(F32)
        done(k, place, columns)


def place_left_kernel(place_ref, *refs):
    pieces, (query_ref, key_ref, value_ref, proj_ref, gain_ref, up_ref, full, sems) = refs[:5], refs[5:]
    copies = []

    def send(k, place, columns):
        copies.append(pltpu.make_async_copy(full.at[pl.ds(0, ROWS), columns], up_ref.at[:, columns], sems.at[k]))
        copies[-1].start()

    place_all(place_ref[0], place_ref[1], pieces, full, send)
    rows = slice(ROWS + 16, 2 * ROWS + 16)
    query_ref[...] = full[rows, :D]
    key_ref[...] = full[rows, D:QK].T
    value_ref[...] = full[rows, QK:QKV].T
    proj_ref[...] = full[rows, QKV:]
    gain_ref[...] = full[2 * ROWS + 16 : 2 * ROWS + 24, :256]
    wait_all(copies)


def place_right_kernel(place_ref, *refs):
    pieces, (gate_ref, down_ref, full, sems) = refs[:5], refs[5:]
    copies = []

    def send(k, place, columns):
        rows = pl.ds(pl.multiple_of(place * ROWS, 16), ROWS)
        copies.append(pltpu.make_async_copy(full.at[pl.ds(0, ROWS), columns], gate_ref.at[:, columns], sems.at[0, k]))
        copies.append(pltpu.make_async_copy(full.at[pl.ds(ROWS + 16, ROWS), columns], down_ref.at[rows], sems.at[1, k]))
        start_all(copies[-2:])

    place_all(place_ref[1], place_ref[0], pieces, full, send)
    wait_all(copies)


def run(kernel, name, ins, specs, outs, scratch, flops, out_specs=None):
    moved = sum(a.size * a.dtype.itemsize for a in ins) + sum(o.size * o.dtype.itemsize for o in outs)
    return pl.pallas_call(
        kernel,
        name=name,
        out_shape=outs,
        in_specs=specs,
        out_specs=out_specs or [VMEM] * len(outs),
        scratch_shapes=scratch,
        cost_estimate=pl.CostEstimate(flops=flops, bytes_accessed=moved, transcendentals=0),
        compiler_params=pltpu.CompilerParams(vmem_limit_bytes=LIMIT),
    )(*ins)


def swap_cores(value):
    return lax.ppermute(value, "core", [(0, 1), (1, 0)])


def shift_y(value, by):
    place = [(y % 2) * 2 + y // 2 for y in range(4)]
    return lax.ppermute(value, ("y_lo", "y_hi"), [(place[y], place[(y + by) % 4]) for y in range(4)])


def in_order(parts):
    core = lax.axis_index("core") == 1
    low = lax.axis_index("y_lo") == 1
    near = [jnp.where(core, parts[k ^ 1], parts[k]) for k in range(4)]
    return jnp.stack([jnp.where(low, near[k ^ 2], near[k]) for k in range(4)])


def after(value, *others):
    return lax.optimization_barrier((value, *others))[0]


def add_low(*terms):
    total = terms[0].astype(F32)
    for term in terms[1:]:
        total = total + term.astype(F32)
    return total.astype(BF)


def shift_ring(value, axis, by):
    return lax.ppermute(value, axis, [(i, (i + by) % 4) for i in range(4)])


def halves(value):
    half = value.shape[0] // 2
    return value[:half], value[half:]


def ring_scatter(*parts):
    sent = []
    for value, axis in parts:
        place = lax.axis_index(axis)
        own, before, behind, across = [
            lax.dynamic_index_in_dim(value, lax.rem(place + by, 4), 0, keepdims=False) for by in (0, 3, 1, 2)
        ]
        top, bottom = halves(across)
        sent.append((axis, own, before, behind, shift_ring(top, axis, 1), shift_ring(bottom, axis, -1)))
    moved = []
    for axis, own, before, behind, top, bottom in sent:
        behind = jnp.concatenate([add_low(halves(behind)[0], top), halves(behind)[1]])
        before = jnp.concatenate([halves(before)[0], add_low(halves(before)[1], bottom)])
        moved.append((own, shift_ring(behind, axis, 1), shift_ring(before, axis, -1)))
    return [add_low(*terms) for terms in moved]


def ring_gather(*parts):
    first = [(value, axis, shift_ring(value, axis, 1), shift_ring(value, axis, -1)) for value, axis in parts]
    return [
        [value, before, behind, shift_ring(halves(before)[0], axis, 1), shift_ring(halves(behind)[1], axis, -1)]
        for value, axis, before, behind in first
    ]


def body(tokens, lengths, norm_attn, w_query, w_key, w_value, w_out, norm_mlp, w_gate, w_up, w_down, cotangent):
    low, core = lax.axis_index("y_lo"), lax.axis_index("core")
    me = (low * 2 + core).astype(jnp.int32)[None]
    first = [jnp.concatenate([w_query, w_key], axis=1), jnp.concatenate([w_out, w_value], axis=1)]
    far = [shift_y(first[0], 1), shift_y(first[1], -1)]
    near = [swap_cores(m) for m in first]
    own_gains = jnp.stack([norm_attn, norm_mlp])
    far_gains = shift_y(own_gains, 1)
    pair = jnp.stack([own_gains, far_gains])
    other = swap_cores(pair)
    gains = in_order([pair[0], other[0], pair[1], other[1]]).transpose(1, 0, 2).reshape(2, D).astype(F32)
    first = [piece for k in range(2) for piece in (first[k], near[k], far[k], swap_cores(far[k]))]
    near_wide = swap_cores(w_gate), swap_cores(w_up)
    near_down = swap_cores(w_down.T)
    held_gate, held_up = lax.optimization_barrier((w_gate, w_up, *far, other, near_down, *near_wide))[:2]
    far_gate, far_up = shift_y(held_gate, 1), shift_y(held_up, -1)

    slots = jnp.arange(T, dtype=jnp.int32)
    ends = jnp.cumsum(lengths[0])
    start = jnp.max(jnp.where(slots[:, None] >= ends[None, :], ends[None, :], 0), axis=1)
    freq = BASE ** (-jnp.arange(HEAD_DIM // 2, dtype=F32) * 2.0 / HEAD_DIM)
    angle = (slots - start).astype(F32)[:, None] * freq[None, :]
    cosine = jnp.tile(jnp.cos(angle), (1, 4))
    sine = jnp.sin(angle)
    sine = jnp.tile(jnp.concatenate([-sine, sine], axis=1), (1, 2))
    start = start[:, None]

    dma = pltpu.SemaphoreType.DMA
    q, k, v, p0, p1, p2, x, h, b_low, *turned = run(
        attention_kernel,
        "attention",
        (me, tokens[0].T, gains, cosine, sine, start, *first),
        [SMEM] + [VMEM] * 5 + [ANY] * 8,
        [
            shape(KV, GROUP * T, HEAD_DIM),
            shape(KV, T, HEAD_DIM),
            shape(KV, T, HEAD_DIM),
            *(shape(KV, STACK, BLOCK * (i + 1)) for i in range(BLOCKS)),
            shape(T, D),
            shape(T, D, dtype=F32),
            shape(T, D),
            *[shape(D, T)] * 3,
        ],
        [pltpu.VMEM((D, PACK), BF), pltpu.VMEM((KV, GROUP * T, HEAD_DIM), F32), pltpu.VMEM((T, T), F32), pltpu.VMEM((T, D), BF), dma((2, 4))],
        2 * T * D * 2560 + 4 * HEADS * T * T * 128,
    )
    held_down = after(w_down.T, b_low)
    far_down = (shift_y(held_down[: D // 2], 1), shift_y(held_down[D // 2 :], -1))
    held = [swap_cores(after(part, b_low)) for part in (far_gate, far_up)]
    wide = [w_gate, near_wide[0], far_gate, held[0], w_up, near_wide[1], far_up, held[1]]
    act, silu, slope = run(
        gate_kernel,
        "gate_up",
        (me, b_low, *wide),
        [SMEM, VMEM] + [ANY] * 8,
        [shape(T, FF)] * 3,
        [pltpu.VMEM((D, 2 * FF), BF), dma((2 * FF // CHUNK, 4))],
        4 * T * D * FF,
    )
    down = [w_down.T, near_down, *far_down, *(swap_cores(after(part, act)) for part in far_down)]
    down_blocks = run(
        down_grad_kernel,
        "down_grad",
        (me, cotangent[0].T, act, *far_down),
        [SMEM, VMEM, VMEM, ANY, ANY],
        [shape(4, ROWS + 16, UNIT)] * 4,
        [pltpu.VMEM((4, 4, ROWS, UNIT), BF), dma((4, 4))],
        2 * T * D * FF,
        [ANY] * 4,
    )
    down_got = [swap_cores(down_blocks[k]) for k in range(2)]
    down_theirs = [add_low(down_blocks[2][part], down_got[0][part]) for part in (slice(0, 2), slice(2, 4))]
    down_y = [shift_y(down_theirs[0], 1), shift_y(down_theirs[1], -1)]
    result, d_gate, d_up, d_h, d_low, d_gain_mlp = run(
        mlp_kernel,
        "mlp_back",
        (me, act, silu, slope, h, cotangent[0].T, gains, *down, *wide, *down_theirs),
        [SMEM] + [VMEM] * 6 + [ANY] * 16,
        [shape(T, D), shape(T, FF), shape(T, FF), shape(T, D, dtype=F32), shape(T, D), shape(1, D, dtype=F32)],
        [pltpu.VMEM((D, FF), BF), pltpu.VMEM((D, 2 * FF), BF), pltpu.VMEM((T, D), F32), dma((3, 6))],
        8 * T * D * FF,
    )
    wide_blocks, wide_got, held = [], [], down_y
    for name, d_part in (("gate_grad", d_gate), ("up_grad", d_up)):
        blocks = run(
            wide_grad_kernel,
            name,
            (me, turned[2], d_part, *held),
            [SMEM] + [VMEM] * 2 + [ANY] * len(held),
            [shape(4, ROWS + 16, UNIT)] * 4,
            [pltpu.VMEM((4, D, UNIT), BF), dma((4, 4))],
            2 * T * D * FF,
            [ANY] * 4,
        )
        wide_blocks.append(blocks)
        wide_got.append([swap_cores(blocks[k]) for k in range(2)])
        held = blocks[:1]
    wide_theirs = [
        [add_low(wide_blocks[k][2][part], wide_got[k][0][part]) for part in (slice(0, 2), slice(2, 4))] for k in range(2)
    ]
    wide_y = [[shift_y(parts[0], 1), shift_y(parts[1], -1)] for parts in wide_theirs]
    d_qkv, grad_input, d_gain_attn = run(
        attention_back_kernel,
        "attention_back",
        (me, x, gains, cosine, sine, d_low, d_h, q, k, v, p0, p1, p2, *first, *wide_theirs[0]),
        [SMEM] + [VMEM] * 12 + [ANY] * 10,
        [shape(T, QKV), shape(T, D, dtype=F32), shape(1, D, dtype=F32)],
        [
            pltpu.VMEM((D, PACK), BF),
            pltpu.VMEM((KV, GROUP * T, HEAD_DIM), BF),
            pltpu.VMEM((KV, GROUP * T, HEAD_DIM), F32),
            pltpu.VMEM((KV, T, HEAD_DIM), F32),
            pltpu.VMEM((KV, T, HEAD_DIM), F32),
            dma((2, 4)),
        ],
        2 * T * D * 2560 + 8 * HEADS * T * T * 128,
    )
    d_gains = jnp.concatenate([d_gain_attn, d_gain_mlp]).reshape(2, 4, ROWS).transpose(1, 0, 2)
    d_gains = jnp.pad(d_gains, ((0, 0), (0, 14), (0, UNIT - ROWS))).astype(BF)
    first_blocks = run(
        attention_grad_kernel,
        "attention_grad",
        (me, *turned[:2], d_qkv, d_low, d_gains, *wide_y[0], *wide_theirs[1]),
        [SMEM] + [VMEM] * 5 + [ANY] * 4,
        [shape(4, ROWS + 16, UNIT)] * 4,
        [pltpu.VMEM((4, D, UNIT), BF), dma((4, 4)), dma((4,))],
        2 * T * D * FF,
        [ANY] * 4,
    )
    first_got = [swap_cores(first_blocks[k]) for k in range(2)]
    first_theirs = [add_low(first_blocks[2][part], first_got[0][part]) for part in (slice(0, 2), slice(2, 4))]
    first_y = [shift_y(first_theirs[0], 1), shift_y(first_theirs[1], -1)]
    wide_y[1] = [after(part, first_theirs[0]) for part in wide_y[1]]
    sum_gate, sum_up = [add_low(wide_blocks[k][3], wide_got[k][1], jnp.concatenate(wide_y[k])) for k in range(2)]
    sum_down = add_low(down_blocks[3], down_got[1], after(jnp.concatenate(down_y), first_theirs[0]))
    sum_first = add_low(first_blocks[3], first_got[1], jnp.concatenate(first_y))
    result, grad_input, sum_first = lax.optimization_barrier((result.T, grad_input.T, sum_first))
    left = jnp.concatenate([sum_up, sum_first], axis=1)
    right = jnp.concatenate([sum_gate, sum_down], axis=1)
    left, right = ring_scatter((left, "z"), (right, "x"))
    left, right = ring_scatter((left.reshape(4, -1, UNIT), "x"), (right.reshape(4, -1, UNIT), "z"))
    both = jnp.stack([left, right])
    left, right = add_low(both, lax.ppermute(both, "y_hi", [(0, 1), (1, 0)]))
    left, right = ring_gather((left, "x"), (right, "z"))
    left, right = ring_gather((jnp.concatenate(left), "z"), (jnp.concatenate(right), "x"))

    places = jnp.stack([lax.axis_index("z"), lax.axis_index("x")]).astype(jnp.int32)
    specs = [SMEM] + [VMEM] * 5
    gate, down_grad = run(
        place_right_kernel,
        "place_gate_down",
        (places, *right),
        specs,
        [shape(ROWS, FF, dtype=F32), shape(D, UNIT, dtype=F32)],
        [pltpu.VMEM((2 * (ROWS + 16), FF), F32), dma((2, 4))],
        0,
        [ANY] * 2,
    )
    query, key, value, proj, gain, up = run(
        place_left_kernel,
        "place_up_attention",
        (places, *left),
        specs,
        [
            shape(ROWS, D, dtype=F32),
            shape(KV * HEAD_DIM, ROWS, dtype=F32),
            shape(KV * HEAD_DIM, ROWS, dtype=F32),
            shape(ROWS, D, dtype=F32),
            shape(8, 256, dtype=F32),
            shape(ROWS, FF, dtype=F32),
        ],
        [pltpu.VMEM((2 * (ROWS + 16), FF), F32), dma((4,))],
        0,
        [VMEM] * 5 + [ANY],
    )
    down_grad = down_grad.T
    return (result.T[None], grad_input.T[None], gain[0, :ROWS], query, key.T, value.T, proj, gain[1, :ROWS], gate, up, down_grad)


def solution(mesh):
    torus = Mesh(mesh.devices.reshape(2, 2, 4, 4, 2), EVERY)
    rows = P(EVERY, None, None)
    weight = P(SHARD, None)
    gain = P(SHARD)
    return jax.shard_map(
        body,
        mesh=torus,
        in_specs=(rows, P(EVERY, None), gain, weight, weight, weight, weight, gain, weight, weight, weight, rows),
        out_specs=(rows, rows, gain, weight, weight, weight, weight, gain, weight, weight, weight),
        check_vma=False,
    )
```

```python
import jax
import jax.numpy as jnp
from jax import lax
from jax.experimental import pallas as pl
from jax.experimental.pallas import tpu as pltpu
from jax.sharding import Mesh
from jax.sharding import PartitionSpec as P

T = 384
D = 960
FF = 2560
HEADS = 15
KV = 5
GROUP = 3
HEAD_DIM = 64
BLOCK = 128
BLOCKS = T // BLOCK
STACK = GROUP * BLOCK
QK = (HEADS + KV) * HEAD_DIM
QKV = QK + KV * HEAD_DIM
PACK = 2 * QK
ROWS = D // 4
UNIT = 640
EVERY = ("y_lo", "core", "z", "x", "y_hi")
SHARD = ("y_lo", "core")
EPS = 1e-05
BASE = 100000.0
MASKED = -1e30
BF = jnp.bfloat16
F32 = jnp.float32
LIMIT = 52 * 2**20

ANY = pl.BlockSpec(memory_space=pl.ANY)
VMEM = pl.BlockSpec(memory_space=pltpu.VMEM)
SMEM = pl.BlockSpec(memory_space=pltpu.SMEM)


def shape(*dims, dtype=BF):
    return jax.ShapeDtypeStruct(dims, dtype)


def mult(left, right):
    return jnp.dot(left, right, preferred_element_type=F32)


def mult_tn(left, right):
    return lax.dot_general(left, right, (((0,), (0,)), ((), ())), preferred_element_type=F32)


def mult_nt(left, right):
    return lax.dot_general(left, right, (((1,), (1,)), ((), ())), preferred_element_type=F32)


def shard_at(me, flip, rows, unit):
    return pl.ds(pl.multiple_of(lax.bitwise_xor(me, jnp.int32(flip)) * rows, unit), rows)


def row_copies(pieces, full, me, sems, columns=None, at=0):
    copies = []
    for flip, source in enumerate(pieces):
        width = source.shape[1]
        target = pl.ds(at, width)
        if columns is not None:
            source, target = source.at[:, columns], pl.ds(at + columns.start, columns.size)
        copies.append(pltpu.make_async_copy(source, full.at[shard_at(me, flip, ROWS, 16), target], sems.at[flip]))
    return copies


def column_copies(pieces, full, me, sems):
    copies = []
    for k, (flip, start, size) in enumerate(((0, 0, D), (1, 0, D), (2, 0, D // 2), (2, D // 2, D // 2), (3, 0, D // 2), (3, D // 2, D // 2))):
        target = full.at[pl.ds(start, size), shard_at(me, flip, FF // 4, 128)]
        copies.append(pltpu.make_async_copy(pieces[k], target, sems.at[k]))
    return copies


def start_all(copies):
    for copy in copies:
        copy.start()


def wait_all(copies):
    for copy in copies:
        copy.wait()


def rope(u, cosine, sine, sign):
    lane = lax.broadcasted_iota(jnp.int32, u.shape, 1)
    turned = jnp.where(lane % HEAD_DIM < HEAD_DIM // 2, pltpu.roll(u, 96, 1), pltpu.roll(u, 32, 1))
    return u * cosine + sign * (turned * sine)


def rms_scale(v):
    return lax.rsqrt(jnp.mean(v * v, axis=-1, keepdims=True) + EPS)


def norm_back(v, gain, grad):
    scale = rms_scale(v)
    inner = grad * gain
    d_v = scale * inner - v * (scale * scale * scale) * jnp.mean(v * inner, axis=-1, keepdims=True)
    return d_v, jnp.sum(grad * v * scale, axis=0, keepdims=True)


def attention_kernel(me_ref, x_ref, gains_ref, cos_ref, sin_ref, start_ref, *refs):
    pieces, refs = refs[:8], refs[8:]
    (q_ref, k_ref, v_ref, p0_ref, p1_ref, p2_ref, x_out_ref, h_ref, b_ref, a_turned_ref, att_turned_ref, b_turned_ref, w, o, bias, att_ref, sems) = refs
    copies = row_copies(pieces[:4], w, me_ref[0], sems.at[0])
    copies += row_copies(pieces[4:], w, me_ref[0], sems.at[1], at=QK)
    start_all(copies)
    x_out_ref[...] = x_ref[...].T
    x = x_out_ref[...].astype(F32)
    a = (x * rms_scale(x) * gains_ref[0:1]).astype(BF)
    a_turned_ref[...] = a.T
    column = lax.broadcasted_iota(jnp.int32, (T, T), 1)
    row = lax.broadcasted_iota(jnp.int32, (T, T), 0)
    bias[...] = jnp.where((column >= start_ref[...]) & (column <= row), 0.0, MASKED)
    wait_all(copies)
    for c in range(QK // 256):
        wide = mult(a, w[:, 256 * c : 256 * (c + 1)])
        for half in range(2):
            u = rope(wide[:, 128 * half : 128 * half + 128], cos_ref[...], sin_ref[...], 1.0).astype(BF)
            for side in range(2):
                head = 4 * c + 2 * half + side
                one = u[:, HEAD_DIM * side : HEAD_DIM * (side + 1)]
                if head < HEADS:
                    for i in range(BLOCKS):
                        at = i * STACK + head % GROUP * BLOCK
                        q_ref[head // GROUP, at : at + BLOCK, :] = one[i * BLOCK : (i + 1) * BLOCK]
                else:
                    k_ref[head - HEADS] = one
    values = mult(a, w[:, QK + D :]).astype(BF)
    for j in range(KV):
        v_ref[j] = values[:, HEAD_DIM * j : HEAD_DIM * (j + 1)]
    probs = (p0_ref, p1_ref, p2_ref)

    def one_group(j, carry):
        for i in range(BLOCKS):
            keys = (i + 1) * BLOCK
            q = q_ref[j, i * STACK : (i + 1) * STACK, :]
            scores = mult_nt(q, k_ref[j, :keys, :]) * 0.125
            part = bias[i * BLOCK : (i + 1) * BLOCK, :keys]
            scores = scores + jnp.concatenate([part] * GROUP, axis=0)
            expo = jnp.exp(scores - jnp.max(scores, axis=-1, keepdims=True))
            prob = (expo * (1.0 / jnp.sum(expo, axis=-1, keepdims=True))).astype(BF)
            probs[i][j] = prob
            o[j, i * STACK : (i + 1) * STACK, :] = mult(prob, v_ref[j, :keys, :])
        return carry

    lax.fori_loop(0, KV, one_group, 0, unroll=True)
    for c in range(8):
        heads = [stacked_head(o, head) for head in range(2 * c, min(2 * c + 2, HEADS))]
        wide = jnp.concatenate(heads, axis=1) if len(heads) > 1 else heads[0]
        att_ref[:, 128 * c : 128 * c + wide.shape[1]] = wide.astype(BF)
    att = att_ref[...]
    att_turned_ref[...] = att.T
    h = x_out_ref[...].astype(F32) + mult(att, w[:, QK : QK + D])
    h_ref[...] = h
    b = (h * rms_scale(h) * gains_ref[1:2]).astype(BF)
    b_ref[...] = b
    b_turned_ref[...] = b.T


def stacked_head(ref, head):
    at = head % GROUP * BLOCK
    return jnp.concatenate(
        [ref[head // GROUP, i * STACK + at : i * STACK + at + BLOCK, :] for i in range(BLOCKS)], axis=0
    )


CHUNK = 512


def gate_kernel(me_ref, b_ref, *refs):
    pieces, (act_ref, silu_ref, slope_ref, w, sems) = refs[:8], refs[8:]
    chunks = FF // CHUNK
    copies = []
    for c in range(chunks):
        for k in range(2):
            part = pieces[4 * k : 4 * k + 4]
            copies.append(row_copies(part, w, me_ref[0], sems.at[2 * c + k], pl.ds(c * CHUNK, CHUNK), k * FF))
    for group in copies:
        start_all(group)
    b = b_ref[...]
    for c in range(chunks):
        at = c * CHUNK
        for group in copies[2 * c : 2 * c + 2]:
            wait_all(group)
        gate = mult(b, w[:, at : at + CHUNK])
        up = mult(b, w[:, FF + at : FF + at + CHUNK])
        sigma = jax.nn.sigmoid(gate)
        silu = gate * sigma
        act_ref[:, at : at + CHUNK] = (silu * up).astype(BF)
        silu_ref[:, at : at + CHUNK] = silu.astype(BF)
        slope_ref[:, at : at + CHUNK] = (up * sigma * (1.0 + gate * (1.0 - sigma))).astype(BF)


def mlp_kernel(me_ref, act_ref, silu_ref, slope_ref, h_ref, dy_ref, gains_ref, *refs):
    down, wide, refs = refs[:6], refs[6:14], refs[16:]
    (out_ref, d_gate_ref, d_up_ref, d_h_ref, d_low_ref, d_gain_ref, wd, w, sums, sems) = refs
    first = column_copies(down, wd, me_ref[0], sems.at[0])
    second = row_copies(wide[:4], w, me_ref[0], sems.at[1]) + row_copies(wide[4:], w, me_ref[0], sems.at[2], at=FF)
    start_all(first + second)
    wait_all(first)
    dy = dy_ref[...].T
    out_ref[...] = (h_ref[...] + mult_nt(act_ref[...], wd[...])).astype(BF)
    for c in range(FF // CHUNK):
        at = c * CHUNK
        d_act = mult(dy, wd[:, at : at + CHUNK])
        d_gate_ref[:, at : at + CHUNK] = (d_act * slope_ref[:, at : at + CHUNK].astype(F32)).astype(BF)
        d_up_ref[:, at : at + CHUNK] = (d_act * silu_ref[:, at : at + CHUNK].astype(F32)).astype(BF)
    wait_all(second)
    sums[...] = mult_nt(d_gate_ref[...], w[:, :FF]) + mult_nt(d_up_ref[...], w[:, FF:])
    d_norm, d_gain = norm_back(h_ref[...], gains_ref[1:2], sums[...])
    d_h = dy.astype(F32) + d_norm
    d_h_ref[...] = d_h
    d_low_ref[...] = d_h.astype(BF)
    d_gain_ref[...] = d_gain


def attention_back_kernel(me_ref, x_ref, gains_ref, cos_ref, sin_ref, d_low_ref, d_h_ref, q_ref, k_ref, v_ref, p0_ref, p1_ref, p2_ref, *refs):
    pieces, refs = refs[:8], refs[-9:]
    (d_qkv_ref, grad_ref, d_gain_ref, w, d_o, d_q, d_k, d_v, sems) = refs
    copies = row_copies(pieces[:4], w, me_ref[0], sems.at[0])
    copies += row_copies(pieces[4:], w, me_ref[0], sems.at[1], at=QK)
    start_all(copies)
    wait_all(copies)
    d_low = d_low_ref[...]
    for c in range(3):
        part = mult_nt(d_low, w[320 * c : 320 * (c + 1), QK : QK + D]).astype(BF)
        for side in range(5):
            head = 5 * c + side
            for i in range(BLOCKS):
                at = i * STACK + head % GROUP * BLOCK
                d_o[head // GROUP, at : at + BLOCK, :] = part[i * BLOCK : (i + 1) * BLOCK, HEAD_DIM * side : HEAD_DIM * (side + 1)]
    probs = (p0_ref, p1_ref, p2_ref)

    def one_group(j, carry):
        parts_k, parts_v = [], []
        for i in range(BLOCKS):
            keys = (i + 1) * BLOCK
            stack = slice(i * STACK, (i + 1) * STACK)
            low = probs[i][j]
            d_one = d_o[j, stack, :]
            prob = low.astype(F32)
            d_prob = mult_nt(d_one, v_ref[j, :keys, :])
            inner = jnp.sum(prob * d_prob, axis=-1, keepdims=True)
            d_scores = (prob * (d_prob - inner)).astype(BF)
            d_q[j, stack, :] = mult(d_scores, k_ref[j, :keys, :]) * 0.125
            parts_k.append(mult_tn(d_scores, q_ref[j, stack, :]))
            parts_v.append(mult_tn(low, d_one))
        for i in range(BLOCKS):
            rows = slice(i * BLOCK, (i + 1) * BLOCK)
            d_k[j, rows, :] = sum(part[rows] for part in parts_k[i:]) * 0.125
            d_v[j, rows, :] = sum(part[rows] for part in parts_v[i:])
        return carry

    lax.fori_loop(0, KV, one_group, 0, unroll=True)
    for c in range(QK // 128):
        heads = []
        for head in (2 * c, 2 * c + 1):
            heads.append(stacked_head(d_q, head) if head < HEADS else d_k[head - HEADS])
        u = jnp.concatenate(heads, axis=1)
        d_qkv_ref[:, 128 * c : 128 * (c + 1)] = rope(u, cos_ref[...], sin_ref[...], -1.0).astype(BF)
    for c in range(3):
        heads = [d_v[j] for j in range(2 * c, min(2 * c + 2, KV))]
        wide = jnp.concatenate(heads, axis=1) if len(heads) > 1 else heads[0]
        d_qkv_ref[:, QK + 128 * c : QK + 128 * c + wide.shape[1]] = wide.astype(BF)
    d_a = mult_nt(d_qkv_ref[:, :QK], w[:, :QK]) + mult_nt(d_qkv_ref[:, QK:], w[:, QK + D :])
    d_norm, d_gain = norm_back(x_ref[...].astype(F32), gains_ref[0:1], d_a)
    grad_ref[...] = d_h_ref[...] + d_norm
    d_gain_ref[...] = d_gain


FLIPS = (3, 1, 2, 0)


def block_copies(full, outs, sems, me, chunk):
    return [
        pltpu.make_async_copy(full.at[chunk, shard_at(me, flip, ROWS, 16)], out.at[chunk, pl.ds(0, ROWS)], sems.at[chunk, k])
        for k, (flip, out) in enumerate(zip(FLIPS, outs))
    ]


def down_grad_kernel(me_ref, dy_ref, act_ref, *refs):
    outs, full, sems = refs[-6:-2], refs[-2], refs[-1]
    copies = []
    for k, (flip, out) in enumerate(zip(FLIPS, outs)):
        part = act_ref[:, shard_at(me_ref[0], flip, FF // 4, 128)]
        for c in range(4):
            full[k, c] = mult(dy_ref[ROWS * c : ROWS * (c + 1), :], part).astype(BF)
            copies.append(pltpu.make_async_copy(full.at[k, c], out.at[c, pl.ds(0, ROWS)], sems.at[k, c]))
            copies[-1].start()
    wait_all(copies)


def wide_grad_kernel(me_ref, b_ref, d_ref, *refs):
    outs, full, sems = refs[-6:-2], refs[-2], refs[-1]
    copies = []
    for c in range(4):
        full[c] = mult(b_ref[...], d_ref[:, UNIT * c : UNIT * (c + 1)]).astype(BF)
        copies += block_copies(full, outs, sems, me_ref[0], c)
        start_all(copies[-4:])
    wait_all(copies)


def attention_grad_kernel(me_ref, a_ref, att_ref, d_qkv_ref, d_low_ref, gain_ref, *refs):
    outs, full, sems, gain_sems = refs[-7:-3], refs[-3], refs[-2], refs[-1]
    a, att = a_ref[...], att_ref[...]
    copies = []
    for k, (flip, out) in enumerate(zip(FLIPS, outs)):
        place = lax.bitwise_xor(me_ref[0], jnp.int32(flip))
        copies.append(pltpu.make_async_copy(gain_ref.at[place], out.at[0, pl.ds(ROWS, 16)], gain_sems.at[k]))
    start_all(copies)
    for c in range(4):
        if c < 2:
            block = mult(a, d_qkv_ref[:, UNIT * c : UNIT * (c + 1)])
        elif c == 2:
            block = jnp.concatenate([mult(a, d_qkv_ref[:, 2 * UNIT :]), mult(att, d_low_ref[:, : UNIT // 2])], axis=1)
        else:
            block = mult(att, d_low_ref[:, UNIT // 2 :])
        full[c] = block.astype(BF)
        copies += block_copies(full, outs, sems, me_ref[0], c)
        start_all(copies[-4:])
    wait_all(copies)


def place_all(first_place, second_place, pieces, held, full, done):
    size = full.shape[0] // 4
    for k, by in enumerate((0, 3, 1, 2)):
        wait_all(pieces[k : k + 1] if k < 3 else pieces[3:])
        place = lax.rem(first_place + by, 4)
        columns = pl.ds(pl.multiple_of(place * UNIT, 128), UNIT)
        for j, other in enumerate((0, 3, 1, 2)):
            rows = pl.ds(pl.multiple_of(lax.rem(second_place + other, 4) * size, 16), size)
            full[rows, columns] = held[k, size * j : size * (j + 1), :].astype(F32)
        done(k, place, columns)


def piece_copies(pieces, held, sems):
    half = held.shape[1] // 2
    targets = [held.at[k] for k in range(3)] + [held.at[3, pl.ds(0, half)], held.at[3, pl.ds(half, half)]]
    return [pltpu.make_async_copy(piece, target, sems.at[k]) for k, (piece, target) in enumerate(zip(pieces, targets))]


def place_kernel(place_ref, *refs):
    left, right, refs = refs[:5], refs[5:10], refs[10:]
    (query_ref, key_ref, value_ref, proj_ref, gain_ref, up_ref, gate_ref, down_ref, held, full_left, full_right, sems, out_sems) = refs
    right = piece_copies(right, held.at[1], sems.at[1])
    left = piece_copies(left, held.at[0], sems.at[0])
    start_all(right + left)
    copies = []

    def send_right(k, place, columns):
        rows = pl.ds(pl.multiple_of(place * ROWS, 16), ROWS)
        copies.append(pltpu.make_async_copy(full_right.at[pl.ds(0, ROWS), columns], gate_ref.at[:, columns], out_sems.at[0, k]))
        copies.append(pltpu.make_async_copy(full_right.at[pl.ds(ROWS + 16, ROWS), columns], down_ref.at[rows], out_sems.at[1, k]))
        start_all(copies[-2:])

    def send_left(k, place, columns):
        copies.append(pltpu.make_async_copy(full_left.at[pl.ds(0, ROWS), columns], up_ref.at[:, columns], out_sems.at[2, k]))
        copies[-1].start()

    place_all(place_ref[1], place_ref[0], right, held.at[1], full_right, send_right)
    place_all(place_ref[0], place_ref[1], left, held.at[0], full_left, send_left)
    rows = slice(ROWS + 16, 2 * ROWS + 16)
    query_ref[...] = full_left[rows, :D]
    key_ref[...] = full_left[rows, D:QK].T
    value_ref[...] = full_left[rows, QK:QKV].T
    proj_ref[...] = full_left[rows, QKV:]
    gain_ref[...] = full_left[2 * ROWS + 16 : 2 * ROWS + 24, :256]
    wait_all(copies)


def run(kernel, name, ins, specs, outs, scratch, flops, out_specs=None):
    moved = sum(a.size * a.dtype.itemsize for a in ins) + sum(o.size * o.dtype.itemsize for o in outs)
    return pl.pallas_call(
        kernel,
        name=name,
        out_shape=outs,
        in_specs=specs,
        out_specs=out_specs or [VMEM] * len(outs),
        scratch_shapes=scratch,
        cost_estimate=pl.CostEstimate(flops=flops, bytes_accessed=moved, transcendentals=0),
        compiler_params=pltpu.CompilerParams(vmem_limit_bytes=LIMIT),
    )(*ins)


def swap_cores(value):
    return lax.ppermute(value, "core", [(0, 1), (1, 0)])


def shift_y(value, by):
    place = [(y % 2) * 2 + y // 2 for y in range(4)]
    return lax.ppermute(value, ("y_lo", "y_hi"), [(place[y], place[(y + by) % 4]) for y in range(4)])


def in_order(parts):
    core = lax.axis_index("core") == 1
    low = lax.axis_index("y_lo") == 1
    near = [jnp.where(core, parts[k ^ 1], parts[k]) for k in range(4)]
    return jnp.stack([jnp.where(low, near[k ^ 2], near[k]) for k in range(4)])


def after(value, *others):
    return lax.optimization_barrier((value, *others))[0]


def add_low(*terms):
    total = terms[0].astype(F32)
    for term in terms[1:]:
        total = total + term.astype(F32)
    return total.astype(BF)


def shift_ring(value, axis, by):
    return lax.ppermute(value, axis, [(i, (i + by) % 4) for i in range(4)])


def halves(value):
    half = value.shape[0] // 2
    return value[:half], value[half:]


def ring_scatter(*parts):
    sent = []
    for value, axis in parts:
        place = lax.axis_index(axis)
        own, before, behind, across = [
            lax.dynamic_index_in_dim(value, lax.rem(place + by, 4), 0, keepdims=False) for by in (0, 3, 1, 2)
        ]
        top, bottom = halves(across)
        sent.append((axis, own, before, behind, shift_ring(top, axis, 1), shift_ring(bottom, axis, -1)))
    moved = []
    for axis, own, before, behind, top, bottom in sent:
        behind = jnp.concatenate([add_low(halves(behind)[0], top), halves(behind)[1]])
        before = jnp.concatenate([halves(before)[0], add_low(halves(before)[1], bottom)])
        moved.append((own, shift_ring(behind, axis, 1), shift_ring(before, axis, -1)))
    return [add_low(*terms) for terms in moved]


def ring_gather(*parts):
    first = [(value, axis, shift_ring(value, axis, 1), shift_ring(value, axis, -1)) for value, axis in parts]
    return [
        [value, before, behind, shift_ring(halves(before)[0], axis, 1), shift_ring(halves(behind)[1], axis, -1)]
        for value, axis, before, behind in first
    ]


def body(tokens, lengths, norm_attn, w_query, w_key, w_value, w_out, norm_mlp, w_gate, w_up, w_down, cotangent):
    low, core = lax.axis_index("y_lo"), lax.axis_index("core")
    me = (low * 2 + core).astype(jnp.int32)[None]
    first = [jnp.concatenate([w_query, w_key], axis=1), jnp.concatenate([w_out, w_value], axis=1)]
    far = [shift_y(first[0], 1), shift_y(first[1], -1)]
    near = [swap_cores(m) for m in first]
    own_gains = jnp.stack([norm_attn, norm_mlp])
    far_gains = shift_y(own_gains, 1)
    pair = jnp.stack([own_gains, far_gains])
    other = swap_cores(pair)
    gains = in_order([pair[0], other[0], pair[1], other[1]]).transpose(1, 0, 2).reshape(2, D).astype(F32)
    first = [piece for k in range(2) for piece in (first[k], near[k], far[k], swap_cores(far[k]))]
    near_wide = swap_cores(w_gate), swap_cores(w_up)
    near_down = swap_cores(w_down.T)
    held_gate, held_up = lax.optimization_barrier((w_gate, w_up, *far, other, near_down, *near_wide))[:2]
    far_gate, far_up = shift_y(held_gate, 1), shift_y(held_up, -1)

    slots = jnp.arange(T, dtype=jnp.int32)
    ends = jnp.cumsum(lengths[0])
    start = jnp.max(jnp.where(slots[:, None] >= ends[None, :], ends[None, :], 0), axis=1)
    freq = BASE ** (-jnp.arange(HEAD_DIM // 2, dtype=F32) * 2.0 / HEAD_DIM)
    angle = (slots - start).astype(F32)[:, None] * freq[None, :]
    cosine = jnp.tile(jnp.cos(angle), (1, 4))
    sine = jnp.sin(angle)
    sine = jnp.tile(jnp.concatenate([-sine, sine], axis=1), (1, 2))
    start = start[:, None]

    dma = pltpu.SemaphoreType.DMA
    q, k, v, p0, p1, p2, x, h, b_low, *turned = run(
        attention_kernel,
        "attention",
        (me, tokens[0].T, gains, cosine, sine, start, *first),
        [SMEM] + [VMEM] * 5 + [ANY] * 8,
        [
            shape(KV, GROUP * T, HEAD_DIM),
            shape(KV, T, HEAD_DIM),
            shape(KV, T, HEAD_DIM),
            *(shape(KV, STACK, BLOCK * (i + 1)) for i in range(BLOCKS)),
            shape(T, D),
            shape(T, D, dtype=F32),
            shape(T, D),
            *[shape(D, T)] * 3,
        ],
        [pltpu.VMEM((D, PACK), BF), pltpu.VMEM((KV, GROUP * T, HEAD_DIM), F32), pltpu.VMEM((T, T), F32), pltpu.VMEM((T, D), BF), dma((2, 4))],
        2 * T * D * 2560 + 4 * HEADS * T * T * 128,
    )
    held_down = after(w_down.T, b_low)
    far_down = (shift_y(held_down[: D // 2], 1), shift_y(held_down[D // 2 :], -1))
    held = [swap_cores(after(part, b_low)) for part in (far_gate, far_up)]
    wide = [w_gate, near_wide[0], far_gate, held[0], w_up, near_wide[1], far_up, held[1]]
    act, silu, slope = run(
        gate_kernel,
        "gate_up",
        (me, b_low, *wide),
        [SMEM, VMEM] + [ANY] * 8,
        [shape(T, FF)] * 3,
        [pltpu.VMEM((D, 2 * FF), BF), dma((2 * FF // CHUNK, 4))],
        4 * T * D * FF,
    )
    down = [w_down.T, near_down, *far_down, *(swap_cores(after(part, act)) for part in far_down)]
    down_blocks = run(
        down_grad_kernel,
        "down_grad",
        (me, cotangent[0].T, act, *far_down),
        [SMEM, VMEM, VMEM, ANY, ANY],
        [shape(4, ROWS + 16, UNIT)] * 4,
        [pltpu.VMEM((4, 4, ROWS, UNIT), BF), dma((4, 4))],
        2 * T * D * FF,
        [ANY] * 4,
    )
    down_got = [swap_cores(down_blocks[k]) for k in range(2)]
    down_theirs = [add_low(down_blocks[2][part], down_got[0][part]) for part in (slice(0, 2), slice(2, 4))]
    down_y = [shift_y(down_theirs[0], 1), shift_y(down_theirs[1], -1)]
    result, d_gate, d_up, d_h, d_low, d_gain_mlp = run(
        mlp_kernel,
        "mlp_back",
        (me, act, silu, slope, h, cotangent[0].T, gains, *down, *wide, *down_theirs),
        [SMEM] + [VMEM] * 6 + [ANY] * 16,
        [shape(T, D), shape(T, FF), shape(T, FF), shape(T, D, dtype=F32), shape(T, D), shape(1, D, dtype=F32)],
        [pltpu.VMEM((D, FF), BF), pltpu.VMEM((D, 2 * FF), BF), pltpu.VMEM((T, D), F32), dma((3, 6))],
        8 * T * D * FF,
    )
    wide_blocks, wide_got, held = [], [], down_y
    for name, d_part in (("gate_grad", d_gate), ("up_grad", d_up)):
        blocks = run(
            wide_grad_kernel,
            name,
            (me, turned[2], d_part, *held),
            [SMEM] + [VMEM] * 2 + [ANY] * len(held),
            [shape(4, ROWS + 16, UNIT)] * 4,
            [pltpu.VMEM((4, D, UNIT), BF), dma((4, 4))],
            2 * T * D * FF,
            [ANY] * 4,
        )
        wide_blocks.append(blocks)
        wide_got.append([swap_cores(blocks[k]) for k in range(2)])
        held = blocks[:1]
    wide_theirs = [
        [add_low(wide_blocks[k][2][part], wide_got[k][0][part]) for part in (slice(0, 2), slice(2, 4))] for k in range(2)
    ]
    wide_y = [[shift_y(parts[0], 1), shift_y(parts[1], -1)] for parts in wide_theirs]
    d_qkv, grad_input, d_gain_attn = run(
        attention_back_kernel,
        "attention_back",
        (me, x, gains, cosine, sine, d_low, d_h, q, k, v, p0, p1, p2, *first, *wide_theirs[0]),
        [SMEM] + [VMEM] * 12 + [ANY] * 10,
        [shape(T, QKV), shape(T, D, dtype=F32), shape(1, D, dtype=F32)],
        [
            pltpu.VMEM((D, PACK), BF),
            pltpu.VMEM((KV, GROUP * T, HEAD_DIM), BF),
            pltpu.VMEM((KV, GROUP * T, HEAD_DIM), F32),
            pltpu.VMEM((KV, T, HEAD_DIM), F32),
            pltpu.VMEM((KV, T, HEAD_DIM), F32),
            dma((2, 4)),
        ],
        2 * T * D * 2560 + 8 * HEADS * T * T * 128,
    )
    d_gains = jnp.concatenate([d_gain_attn, d_gain_mlp]).reshape(2, 4, ROWS).transpose(1, 0, 2)
    d_gains = jnp.pad(d_gains, ((0, 0), (0, 14), (0, UNIT - ROWS))).astype(BF)
    first_blocks = run(
        attention_grad_kernel,
        "attention_grad",
        (me, *turned[:2], d_qkv, d_low, d_gains, *wide_y[0], *wide_theirs[1]),
        [SMEM] + [VMEM] * 5 + [ANY] * 4,
        [shape(4, ROWS + 16, UNIT)] * 4,
        [pltpu.VMEM((4, D, UNIT), BF), dma((4, 4)), dma((4,))],
        2 * T * D * FF,
        [ANY] * 4,
    )
    first_got = [swap_cores(first_blocks[k]) for k in range(2)]
    first_theirs = [add_low(first_blocks[2][part], first_got[0][part]) for part in (slice(0, 2), slice(2, 4))]
    first_y = [shift_y(first_theirs[0], 1), shift_y(first_theirs[1], -1)]
    wide_y[1] = [after(part, first_theirs[0]) for part in wide_y[1]]
    sum_gate, sum_up = [add_low(wide_blocks[k][3], wide_got[k][1], jnp.concatenate(wide_y[k])) for k in range(2)]
    sum_down = add_low(down_blocks[3], down_got[1], after(jnp.concatenate(down_y), first_theirs[0]))
    sum_first = add_low(first_blocks[3], first_got[1], jnp.concatenate(first_y))
    result, grad_input, sum_first = lax.optimization_barrier((result.T, grad_input.T, sum_first))
    left = jnp.concatenate([sum_up, sum_first], axis=1)
    right = jnp.concatenate([sum_gate, sum_down], axis=1)
    left, right = ring_scatter((left, "z"), (right, "x"))
    left, right = ring_scatter((left.reshape(4, -1, UNIT), "x"), (right.reshape(4, -1, UNIT), "z"))
    both = jnp.stack([left, right])
    left, right = add_low(both, lax.ppermute(both, "y_hi", [(0, 1), (1, 0)]))
    left, right = ring_gather((left, "x"), (right, "z"))
    left, right = ring_gather((jnp.concatenate(left), "z"), (jnp.concatenate(right), "x"))

    places = jnp.stack([lax.axis_index("z"), lax.axis_index("x")]).astype(jnp.int32)
    query, key, value, proj, gain, up, gate, down_grad = run(
        place_kernel,
        "place_gradients",
        (places, *left, *right),
        [SMEM] + [ANY] * 10,
        [
            shape(ROWS, D, dtype=F32),
            shape(KV * HEAD_DIM, ROWS, dtype=F32),
            shape(KV * HEAD_DIM, ROWS, dtype=F32),
            shape(ROWS, D, dtype=F32),
            shape(8, 256, dtype=F32),
            shape(ROWS, FF, dtype=F32),
            shape(ROWS, FF, dtype=F32),
            shape(D, UNIT, dtype=F32),
        ],
        [
            pltpu.VMEM((2, 4, 2 * (ROWS + 16), UNIT), BF),
            pltpu.VMEM((2 * (ROWS + 16), FF), F32),
            pltpu.VMEM((2 * (ROWS + 16), FF), F32),
            dma((2, 5)),
            dma((3, 4)),
        ],
        0,
        [VMEM] * 5 + [ANY] * 3,
    )
    down_grad = down_grad.T
    return (result.T[None], grad_input.T[None], gain[0, :ROWS], query, key.T, value.T, proj, gain[1, :ROWS], gate, up, down_grad)


def solution(mesh):
    torus = Mesh(mesh.devices.reshape(2, 2, 4, 4, 2), EVERY)
    rows = P(EVERY, None, None)
    weight = P(SHARD, None)
    gain = P(SHARD)
    return jax.shard_map(
        body,
        mesh=torus,
        in_specs=(rows, P(EVERY, None), gain, weight, weight, weight, weight, gain, weight, weight, weight, rows),
        out_specs=(rows, rows, gain, weight, weight, weight, weight, gain, weight, weight, weight),
        check_vma=False,
    )
```
